128 devices in a mesh: row: 8 (over z, core), col: 16 (over y, x).
Axes of the slice: x: 4, y: 4, z: 4, core: 2. Of those that a mesh axis runs over, the one named last changes fastest.
Arguments:
- rhs_held: float32 [393216, 64], P(('row', 'col')), may hold values from -6 to 6
- row_map: int32 [393216], P(('row', 'col')), may hold values from 0 to 393215, as said below
- sep_rhs: float32 [128, 256, 64], P(('row', 'col')), may hold values from -6 to 6
- sep_inverse: float32 [128, 256, 256], P(('row', 'col')), as said below
- sep_parent: float32 [128, 256, 256], P(('row', 'col')), may hold values from -0.1875 to 0.1875
- leaf_inverse: float32 [128, 12, 256, 256], P(('row', 'col')), as said below
- leaf_coupling: float32 [128, 12, 4, 256, 256], P(('row', 'col')), may hold values from -0.1875 to 0.1875
- leaf_links: int32 [128, 12, 4], P(('row', 'col')), may hold values from 0 to 6, as said below
Outputs:
- x_held: float32 [393216, 64], P(('row', 'col'))
- sep_solution: float32 [128, 256, 64], P(('row', 'col'))
The draws below stay inside these ranges and needn't reach their ends.
Inputs may be any that keep to these rules, and one draw needn't show every extreme that they name: `row_map`: a permutation of all leaf rows; every device holds exactly 24 rows of each device's leaf unknowns. `leaf_links`: the 4 entries of one leaf supernode differ; the first leaf supernode of every device couples to the root, distance 7 - 1. `sep_inverse`: upper triangular, diagonal entries positive. `leaf_inverse`: upper triangular, diagonal entries positive.
All inputs are finite; a program needn't handle non-finite values.
Results may differ from the reference program's by a relative error of at most 0.0003.
Values sent between devices are 32-bit elements; how exact they have to be, the bound alone decides.
A program may use at most 128 MiB of HBM per device.

```python
import jax
import jax.numpy as jnp
import numpy as np
from jax import lax

W = 256
NRHS = 64
LEAF = 12
NCOUP = 4
LEVELS = 7
ANCS = 7
ROWS_DEV = 3072
SEG = 24
N_ROW = 8
N_COL = 16
DEVICES = 128


def assemble(diagonal, upper_part):
    rows_idx = lax_rows(upper_part.shape[-1])
    above = rows_idx[:, None] < rows_idx[None, :]
    eye_mat = (rows_idx[:, None] == rows_idx[None, :]).astype(jnp.float32)
    return jnp.where(above, upper_part, 0.0) + diagonal[..., None] * eye_mat


def lax_rows(count):
    return jnp.arange(count)


def draw_sep_inverse(key, part):
    key = jax.random.fold_in(key, 13)
    first, second = jax.random.split(key)
    count = ROWS_DEV // SEG
    diagonal = jax.random.uniform(first, (count, W), jnp.float32, 0.6, 1.6)
    upper_part = 0.7 * jax.random.normal(second, (count, W, W), jnp.float32) / jnp.sqrt(float(W))
    return assemble(diagonal, upper_part)


def draw_leaf_inverse(key, part):
    key = jax.random.fold_in(key, 14)
    first, second = jax.random.split(key)
    count = ROWS_DEV // SEG
    diagonal = jax.random.uniform(first, (count, LEAF, W), jnp.float32, 0.6, 1.6)
    upper_part = 0.7 * jax.random.normal(second, (count, LEAF, W, W), jnp.float32) / jnp.sqrt(float(W))
    return assemble(diagonal, upper_part)


def draw_row_map(key, part):
    key = jax.random.fold_in(key, 11)
    count = ROWS_DEV // SEG
    first, second, third = jax.random.split(key, 3)
    row_perms = jax.vmap(lambda sub: jax.random.permutation(sub, ROWS_DEV))(jax.random.split(first, count))
    global_ids = (row_perms + jnp.arange(count)[:, None] * ROWS_DEV).reshape(count, count, SEG)
    source_perms = jax.vmap(lambda sub: jax.random.permutation(sub, count))(jax.random.split(second, count))
    inverse_perms = jnp.argsort(source_perms, axis=1)
    held = jnp.take_along_axis(global_ids, inverse_perms[:, :, None], axis=1)
    held = jnp.transpose(held, (1, 0, 2)).reshape(count, ROWS_DEV)
    shuffles = jax.vmap(lambda sub: jax.random.permutation(sub, ROWS_DEV))(jax.random.split(third, count))
    held = jnp.take_along_axis(held, shuffles, axis=1)
    return held.reshape(count * ROWS_DEV).astype(jnp.int32)


def draw_leaf_links(key, part):
    key = jax.random.fold_in(key, 12)
    count = ROWS_DEV // SEG
    scores = jax.random.randint(key, (count, LEAF, ANCS), 0, 1024) * ANCS + jnp.arange(ANCS)
    first_leaf = (jnp.arange(LEAF) == 0)[None, :, None]
    root_slot = (jnp.arange(ANCS) == ANCS - 1)[None, None, :]
    scores = jnp.where(first_leaf & root_slot, -1, scores)
    return jnp.argsort(scores, axis=-1)[..., :NCOUP].astype(jnp.int32)


def steps_of(rng, extent, pieces, low, largest):
    factor_of, own = 1.0, jax.random.fold_in(rng, 6)
    for position, blocks in pieces:
        draws = jnp.exp(jax.random.uniform(jax.random.fold_in(own, position), (blocks,), jnp.float32, low / len(pieces), largest / len(pieces)))
        factor_of = factor_of * jnp.repeat(draws, extent[position] // blocks).reshape([-1 if axis == position else 1 for axis in range(len(extent))])
    return factor_of


def normal_values(own_key, extent, width, most, pieces=(), kind=jnp.bfloat16):
    result = width * jax.random.normal(own_key, extent, jnp.float32)
    if pieces:
        result = result * steps_of(own_key, extent, pieces, -0.22, 0.18)
    return jnp.clip(result, -most, most).astype(kind)


def setup_inputs(seed: int = 0) -> dict:
    keys = jax.random.split(jax.random.key(seed), 9)
    rhs_held = normal_values(keys[0], (DEVICES * ROWS_DEV, NRHS), 1.0, 6.0, ((0, 128),), jnp.float32)
    row_map = draw_row_map(jax.random.fold_in(keys[8], 71), 0)
    sep_rhs = normal_values(keys[2], (DEVICES, W, NRHS), 1.0, 6.0, ((0, 128),), jnp.float32)
    sep_inverse = draw_sep_inverse(jax.random.fold_in(keys[8], 71), 0)
    sep_parent = normal_values(keys[4], (DEVICES, W, W), (4 * W) ** -0.5, 0.1875, ((0, 128),), jnp.float32)
    leaf_inverse = draw_leaf_inverse(jax.random.fold_in(keys[8], 71), 0)
    leaf_coupling = normal_values(keys[6], (DEVICES, LEAF, NCOUP, W, W), (4 * W) ** -0.5, 0.1875, ((0, 128),), jnp.float32)
    leaf_links = draw_leaf_links(jax.random.fold_in(keys[8], 71), 0)
    return dict(rhs_held=rhs_held, row_map=row_map, sep_rhs=sep_rhs, sep_inverse=sep_inverse, sep_parent=sep_parent, leaf_inverse=leaf_inverse, leaf_coupling=leaf_coupling, leaf_links=leaf_links)


def owner_of(level_index, node_ids):
    depth = LEVELS - 1 - level_index
    return node_ids * 2 ** (depth + 1) + 2 ** depth - 1


def leaf_solve(inverse, coupling, links, rhs_block, nearest):
    onehot = (links[..., None] == jnp.arange(ANCS)).astype(jnp.float32)
    picked = jnp.einsum("scp,pwr->scwr", onehot, nearest, precision=lax.Precision.HIGHEST)
    contrib = jnp.einsum("scwv,scwr->svr", coupling, picked, precision=lax.Precision.HIGHEST)
    return jnp.einsum("svw,swr->svr", inverse, rhs_block - contrib, precision=lax.Precision.HIGHEST)


def reference(rhs_held, row_map, sep_rhs, sep_inverse, sep_parent, leaf_inverse, leaf_coupling, leaf_links):
    devices = N_ROW * N_COL
    sep_x = jnp.zeros((devices, W, NRHS), jnp.float32)
    for level_index in range(LEVELS):
        node_ids = np.arange(2 ** level_index)
        owners = owner_of(level_index, node_ids)
        target = sep_rhs[owners]
        if level_index > 0:
            parents = owner_of(level_index - 1, node_ids // 2)
            target = target - jnp.einsum("nwv,nwr->nvr", sep_parent[owners], sep_x[parents], precision=lax.Precision.HIGHEST)
        solved = jnp.einsum("nvw,nwr->nvr", sep_inverse[owners], target, precision=lax.Precision.HIGHEST)
        sep_x = sep_x.at[owners].set(solved)
    global_rows = jnp.zeros((devices * ROWS_DEV, NRHS), jnp.float32).at[row_map].set(rhs_held)
    leaf_rhs = global_rows.reshape(devices, LEAF, W, NRHS)
    device_ids = np.arange(devices)
    table = np.stack([(device_ids // 2 ** (p + 1)) * 2 ** (p + 1) + 2 ** p - 1 for p in range(ANCS)], axis=1)
    table = jnp.asarray(table.astype(np.int32))

    def per_device(items):
        inverse, coupling, links, rhs_block, anc_ids = items
        return leaf_solve(inverse, coupling, links, rhs_block, sep_x[anc_ids])

    leaf_x = lax.map(per_device, (leaf_inverse, leaf_coupling, leaf_links, leaf_rhs, table))
    x_held = leaf_x.reshape(devices * ROWS_DEV, NRHS)[row_map]
    return x_held, sep_x
```

```python
import functools

import jax
import jax.numpy as jnp
from jax import lax
from jax.experimental import pallas as pl
from jax.experimental.pallas import tpu as pltpu
from jax.sharding import PartitionSpec as P

MESH = pl.DeviceIdType.MESH
F32 = jnp.float32
BF16 = jnp.bfloat16
I32 = jnp.int32
NN = (((1,), (0,)), ((), ()))
NT = (((1,), (1,)), ((), ()))

DEV = 128
LEVELS = 7
W = 256
R = 64
LEAF = 12
NCOUP = 4
ROWS = 3072
SEG = 24
HALF = 12
MSG = HALF + 1
PITCH = 16


def mesh_id(device):
    return (lax.shift_right_logical(device, 4), device & 15)


def split(value):
    high = value.astype(BF16)
    return high, (value - high.astype(F32)).astype(BF16)


def pieces(x):
    high, low = split(x)
    return jnp.concatenate([high, low], 0), high


def dot3(x2, xh, weights, dims):
    wh, wl = split(weights)
    n = xh.shape[0]
    both = lax.dot_general(x2, wh, dims, preferred_element_type=F32)
    cross = lax.dot_general(xh, wl, dims, preferred_element_type=F32)
    return both[:n] + both[n:] + cross


def iota(shape, axis):
    return lax.broadcasted_iota(I32, shape, axis)


def within(index, size):
    return jnp.clip(index, 0, size - 1)


def onehot(mask):
    return jnp.where(mask, 1.0, 0.0)


def trailing_zeros(number):
    total = jnp.int32(0)
    for k in range(1, 8):
        total = total + jnp.where((number & ((1 << k) - 1)) == 0, 1, 0)
    return total


def gather_pairs(steps, source, table, second, store):
    left = iota((1, 128), 1) < R

    def step(k, carry):
        for l in range(128):
            a = table[first(k), l]
            b = table[second(k), l]
            store(k, l, jnp.where(left, source[pl.ds(a, 1), :], source[pl.ds(b, 1), :]))
        return carry

    first, second = second
    lax.fori_loop(0, steps, step, 0)


def double_halves(value):
    left = iota(value.shape, value.ndim - 1) < R
    swapped = pltpu.roll(value, R, value.ndim - 1)
    return jnp.where(left, value, swapped), jnp.where(left, swapped, value)


def kernel(
    rhs_hbm, map_hbm, seprhs_hbm, sepinv_hbm, seppar_hbm, leafinv_hbm, coup_hbm, links,
    x_hbm, sep_hbm,
    rhs, rmap, seprhs, sepinv, seppar, leafinv, coup,
    doubled, sbuf, rbuf, received, grouped, solved, sbuf2, rbuf2, returned, xout,
    anc, sepout, acc, qt, cums, labels, pos_v, idx_v, idx, idx_r, idx_pos,
    in_sem, loc_sem, tree_send, tree_recv, a_send, a_recv, b_send, b_recv,
):
    me = lax.axis_index("row") * 16 + lax.axis_index("col")

    loads = [
        pltpu.make_async_copy(s, d, in_sem.at[i])
        for i, (s, d) in enumerate(
            (
                (sepinv_hbm, sepinv), (seprhs_hbm, seprhs), (map_hbm, rmap), (seppar_hbm, seppar),
                (rhs_hbm, rhs), (coup_hbm, coup), (leafinv_hbm, leafinv),
            )
        )
    ]
    for load in loads:
        load.start()

    barrier = pltpu.get_barrier_semaphore()

    def greet(k):
        pl.semaphore_signal(barrier, inc=1, device_id=mesh_id(me ^ k), device_id_type=MESH)

    for k in range(1, 8):
        greet(k)

    def greet8(i, carry):
        for k in range(8):
            greet(i * 8 + k)
        return carry

    lax.fori_loop(1, DEV // 8, greet8, 0)

    own = 6 - trailing_zeros(me + 1)
    partner_own = 6 - trailing_zeros(me + 2)
    reach = lax.shift_right_logical(jnp.int32(32), jnp.clip(own, 0, 5))
    inner = (own >= 0) & (own < 6)

    def tree_copy(m, to, which):
        return pltpu.make_async_remote_copy(
            src_ref=anc.at[m], dst_ref=anc.at[m], send_sem=tree_send.at[m, which], recv_sem=tree_recv.at[m],
            device_id=mesh_id(to), device_id_type=MESH,
        )

    def push(m, act):
        @pl.when(inner)
        def _():
            act(tree_copy(m, me - reach, 0))
            act(tree_copy(m, me + reach, 1))

        @pl.when((own == 6) & (m > partner_own))
        def _():
            act(tree_copy(m, me + 1, 0))

    def tree_wait(m):
        tree_copy(m, me, 0).wait_recv()

    def solve_own(m, target):
        t2, th = pieces(target)
        x = dot3(t2, th, sepinv[...], NT)
        anc[m] = x
        sepout[...] = x
        push(m, lambda c: c.start())

    def own_step(m):
        p2, ph = pieces(anc[m - 1])
        solve_own(m, seprhs[...] - dot3(p2, ph, seppar[...], NN))

    loads[0].wait()
    loads[1].wait()
    loads[3].wait()
    pl.semaphore_wait(barrier, DEV - 1)

    @pl.when(own == 0)
    def _():
        solve_own(0, seprhs[...])

    @pl.when(own == 1)
    def _():
        tree_wait(0)
        push(0, lambda c: c.start())
        own_step(1)

    @pl.when(own < 0)
    def _():
        sepout[...] = jnp.zeros_like(sepout)

    loads[2].wait()
    rows = rmap[...]
    dest = lax.shift_right_logical(lax.shift_right_logical(rows, 10) * 171, 9)
    local = rows - dest * ROWS
    for j in range(12):
        for h in range(2):
            r = 2 * j + h
            qt[j * 128:(j + 1) * 128, h * 128:(h + 1) * 128] = onehot(
                iota((128, 128), 0) == dest[r:r + 1, :]
            ).astype(BF16)
    tri = onehot((iota((256, 384), 0) < iota((256, 384), 1)) | (iota((256, 384), 1) >= 256)).astype(BF16)
    cums[...] = lax.dot_general(qt[...], tri, NN, preferred_element_type=F32)
    carry = jnp.zeros((128, 128), F32)
    table = jnp.zeros((128, 128), F32)
    sub32 = iota((32, 128), 0)
    lane = iota((1, 128), 1)
    for j in range(12):
        parts = []
        for h in range(2):
            r = 2 * j + h
            q = qt[j * 128:(j + 1) * 128, h * 128:(h + 1) * 128].astype(F32)
            rank = jnp.sum(q * (cums[j * 128:(j + 1) * 128, h * 128:(h + 1) * 128] + carry), axis=0, keepdims=True)
            rank = rank.astype(I32)
            hit = sub32 == rank
            loc = local[r:r + 1, :]
            parts.append(
                jnp.concatenate(
                    [
                        jnp.where(hit, float(r), 0.0),
                        jnp.where(hit, lane.astype(F32), 0.0),
                        jnp.where(hit, lax.shift_right_logical(loc, 7).astype(F32), 0.0),
                        jnp.where(hit, (loc & 127).astype(F32), 0.0),
                    ],
                    0,
                )
            )
            at = dest[r:r + 1, :] * PITCH + rank + jnp.where(rank >= HALF, DEV * PITCH - HALF, 0)
            pos_v[r:r + 1, :] = within(at, 2 * DEV * PITCH)
        digits = jnp.concatenate(parts, 1).astype(BF16)
        table = table + lax.dot_general(digits, qt[j * 128:(j + 1) * 128, :], NT, preferred_element_type=F32)
        carry = carry + cums[j * 128:(j + 1) * 128, 256:384]
    idx_v[0:24, :] = within((table[0:24] * 128.0 + table[32:56]).astype(I32), ROWS)
    to_idx = pltpu.make_async_copy(idx_v.at[pl.ds(0, 24)], idx, loc_sem.at[0])
    to_idx.start()
    to_pos = pltpu.make_async_copy(pos_v, idx_pos, loc_sem.at[1])
    to_pos.start()
    lab = table[64:96] * 128.0 + table[96:128]
    labels[...] = jnp.concatenate([lab, jnp.zeros((96, 128), F32)], 0).T

    loads[4].wait()

    def double_rhs(j, carry):
        block = rhs[:, pl.ds(pl.multiple_of(j * 128, 128), 128)]
        doubled[pl.ds(pl.multiple_of(j * 128, 128), 128), :] = jnp.concatenate([block, block], 0).T
        return carry

    lax.fori_loop(0, ROWS // 128, double_rhs, 0, unroll=4)

    to_idx.wait()
    to_pos.wait()

    def put_send(k, l, row):
        sbuf[l, pl.ds(k, 1), :] = row

    gather_pairs(HALF, doubled, idx, (lambda k: k, lambda k: k + HALF), put_send)
    for l in range(128):
        sbuf[l, HALF:MSG, :] = labels[l:l + 1, :]

    def exchange(src, dst, send, recv):
        def go(k, carry):
            to = me ^ k
            pltpu.make_async_remote_copy(
                src_ref=src.at[to], dst_ref=dst.at[me], send_sem=send, recv_sem=recv,
                device_id=mesh_id(to), device_id_type=MESH,
            ).start()
            return carry

        lax.fori_loop(1, DEV, go, 0)
        mine = pltpu.make_async_copy(src.at[me], dst.at[me], loc_sem.at[2])
        mine.start()
        mine.wait()

    def exchange_wait(src, dst, sem):
        n = DEV - 1
        pltpu.make_async_copy(src.at[pl.ds(0, n)], dst.at[pl.ds(0, n)], sem).wait()

    exchange(sbuf, rbuf, a_send, a_recv)

    loads[5].wait()
    acc[...] = jnp.zeros_like(acc)

    def level(m, carry):
        @pl.when((m != own) & ((own < 0) | (own > 1) | (m > own)))
        def _():
            tree_wait(m)

        @pl.when((m < own) & (own > 1) | (m > own) & False)
        def _():
            push(m, lambda c: c.start())

        @pl.when((m == own) & (own > 1))
        def _():
            own_step(m)

        p = LEVELS - 1 - m
        x2, xh = pieces(anc[m])

        def blocks(g, c0):
            for u in range(4):
                s = g * 4 + u
                which = jnp.int32(0)
                found = jnp.int32(0)
                for c in range(NCOUP):
                    here = jnp.where(links[s, c] == p, 1, 0)
                    which = jnp.where(here > 0, c, which)
                    found = found + here
                term = dot3(x2, xh, coup[s * NCOUP + which], NN)
                acc[s] += jnp.where(found > 0, term, 0.0)
            return c0

        lax.fori_loop(0, LEAF // 4, blocks, 0)
        return carry

    lax.fori_loop(0, LEVELS, level, 0)

    exchange_wait(sbuf, rbuf, a_recv)
    for p in range(128):
        labels[p:p + 1, :] = rbuf[p, HALF:MSG, :]
    got = labels[...].T[0:32].astype(I32)
    high = lax.shift_right_logical(got, 7)
    low = got & 127
    inverse = jnp.zeros((64, 128), F32)
    for j in range(12):
        aa, bb = [], []
        for h in range(2):
            r = 2 * j + h
            at = lane * PITCH + (r % HALF + (r // HALF) * DEV * PITCH)
            hit = sub32 == high[r:r + 1, :]
            aa.append(
                jnp.concatenate(
                    [
                        jnp.where(hit, lax.shift_right_logical(at, 6).astype(F32), 0.0),
                        jnp.where(hit, (at & 63).astype(F32), 0.0),
                    ],
                    0,
                )
            )
            bb.append(onehot(iota((128, 128), 0) == low[r:r + 1, :]))
        inverse = inverse + lax.dot_general(
            jnp.concatenate(aa, 1).astype(BF16), jnp.concatenate(bb, 1).astype(BF16), NT, preferred_element_type=F32
        )
    idx_v[0:24, :] = within((inverse[0:24] * 64.0 + inverse[32:56]).astype(I32), 2 * DEV * PITCH)
    idx_v[24:48, :] = within(((high & 1) * (ROWS // 2) + lax.shift_right_logical(high, 1) * 128 + low)[0:24], ROWS)
    to_idx = pltpu.make_async_copy(idx_v, idx_r, loc_sem.at[0])
    to_idx.start()

    def double_message(src, dst, n, p):
        lo2, hi2 = double_halves(src[p])
        dst[pl.ds(pl.multiple_of(p * PITCH, PITCH), n), :] = lo2
        dst[pl.ds(pl.multiple_of((p + DEV) * PITCH, PITCH), n), :] = hi2

    def double_received(p, carry):
        double_message(rbuf, received, MSG, p)
        return carry

    lax.fori_loop(0, DEV, double_received, 0, unroll=8)
    to_idx.wait()

    def put_grouped(k, l, row):
        grouped[pl.ds(k * 128 + l, 1), :] = row

    gather_pairs(LEAF, received, idx_r, (lambda k: 2 * k, lambda k: 2 * k + 1), put_grouped)

    loads[6].wait()

    def leaf(g, carry):
        for u in range(4):
            t = g * 4 + u
            at = pl.multiple_of(t * 128, 128)
            both = grouped[pl.ds(at, 128), :].T
            target = jnp.concatenate([both[:R], both[R:]], 1) - acc[t]
            t2, th = pieces(target)
            x = dot3(t2, th, leafinv[t], NT)
            solved[pl.ds(at, 128), :] = jnp.concatenate([x[:, :128], x[:, :128]], 0).T
            solved[pl.ds(pl.multiple_of(at + ROWS // 2, 128), 128), :] = jnp.concatenate([x[:, 128:], x[:, 128:]], 0).T
        return carry

    lax.fori_loop(0, LEAF // 4, leaf, 0)

    def put_back(k, l, row):
        sbuf2[l, pl.ds(k, 1), :] = row

    gather_pairs(HALF, solved, idx_r, (lambda k: k + 24, lambda k: k + 24 + HALF), put_back)
    exchange(sbuf2, rbuf2, b_send, b_recv)
    out_sep = pltpu.make_async_copy(sepout, sep_hbm, loc_sem.at[3])
    out_sep.start()

    exchange_wait(sbuf, rbuf, a_send)

    def settle(m, carry):
        @pl.when(m <= own)
        def _():
            push(m, lambda c: c.wait_send())

        return carry

    lax.fori_loop(0, LEVELS, settle, 0)
    out_sep.wait()

    exchange_wait(sbuf2, rbuf2, b_recv)

    def double_returned(p, carry):
        double_message(rbuf2, returned, HALF, p)
        return carry

    lax.fori_loop(0, DEV, double_returned, 0, unroll=8)

    left = iota((1, 128), 1) < R

    def restore(j, carry):
        for l in range(128):
            a = idx_pos[2 * j, l]
            b = idx_pos[2 * j + 1, l]
            grouped[pl.ds(j * 128 + l, 1), :] = jnp.where(left, returned[pl.ds(a, 1), :], returned[pl.ds(b, 1), :])
        both = grouped[pl.ds(pl.multiple_of(j * 128, 128), 128), :].T
        xout[:, pl.ds(pl.multiple_of(j * 256, 256), 256)] = jnp.concatenate([both[:R], both[R:]], 1)
        return carry

    lax.fori_loop(0, LEAF, restore, 0)
    exchange_wait(sbuf2, rbuf2, b_send)
    out_x = pltpu.make_async_copy(xout, x_hbm, loc_sem.at[0])
    out_x.start()
    out_x.wait()


def per_device(rhs_held, row_map, sep_rhs, sep_inverse, sep_parent, leaf_inverse, leaf_coupling, leaf_links):
    hbm = pl.BlockSpec(memory_space=pltpu.HBM)
    vmem = pltpu.VMEM
    x, sep = pl.pallas_call(
        kernel,
        out_shape=(jax.ShapeDtypeStruct((R, ROWS), F32), jax.ShapeDtypeStruct((R, W), F32)),
        in_specs=[hbm] * 7 + [pl.BlockSpec(memory_space=pltpu.SMEM)],
        out_specs=(hbm, hbm),
        scratch_shapes=[
            vmem((R, ROWS), F32),
            vmem((24, 128), I32),
            vmem((R, W), F32),
            vmem((W, W), F32),
            vmem((W, W), F32),
            vmem((LEAF, W, W), F32),
            vmem((LEAF * NCOUP, W, W), F32),
            vmem((ROWS, 128), F32),
            vmem((DEV, MSG, 128), F32),
            vmem((DEV, MSG, 128), F32),
            vmem((2 * DEV * PITCH, 128), F32),
            vmem((ROWS // 2, 128), F32),
            vmem((ROWS, 128), F32),
            vmem((DEV, HALF, 128), F32),
            vmem((DEV, HALF, 128), F32),
            vmem((2 * DEV * PITCH, 128), F32),
            vmem((R, ROWS), F32),
            vmem((LEVELS, R, W), F32),
            vmem((R, W), F32),
            vmem((LEAF, R, W), F32),
            vmem((12 * 128, 256), BF16),
            vmem((12 * 128, 384), F32),
            vmem((128, 128), F32),
            vmem((24, 128), I32),
            vmem((48, 128), I32),
            pltpu.SMEM((24, 128), I32),
            pltpu.SMEM((48, 128), I32),
            pltpu.SMEM((24, 128), I32),
            pltpu.SemaphoreType.DMA((7,)),
            pltpu.SemaphoreType.DMA((4,)),
            pltpu.SemaphoreType.DMA((LEVELS, 2)),
            pltpu.SemaphoreType.DMA((LEVELS,)),
            pltpu.SemaphoreType.DMA,
            pltpu.SemaphoreType.DMA,
            pltpu.SemaphoreType.DMA,
            pltpu.SemaphoreType.DMA,
        ],
        compiler_params=pltpu.CompilerParams(
            collective_id=0, has_side_effects=True, vmem_limit_bytes=56 << 20
        ),
        name="gmrf_solve",
    )(
        rhs_held.T,
        row_map.reshape(24, 128),
        sep_rhs[0].T,
        sep_inverse[0],
        sep_parent[0],
        leaf_inverse[0],
        leaf_coupling[0].reshape(LEAF * NCOUP, W, W),
        leaf_links[0],
    )
    return x.T, sep.T[None]


def solution(mesh):
    in_specs = (
        P(("row", "col"), None),
        P(("row", "col")),
        P(("row", "col"), None, None),
        P(("row", "col"), None, None),
        P(("row", "col"), None, None),
        P(("row", "col"), None, None, None),
        P(("row", "col"), None, None, None, None),
        P(("row", "col"), None, None),
    )
    out_specs = (P(("row", "col"), None), P(("row", "col"), None, None))
    return jax.shard_map(per_device, mesh=mesh, in_specs=in_specs, out_specs=out_specs, check_vma=False)
```

```python
import functools

import jax
import jax.numpy as jnp
from jax import lax
from jax.experimental import pallas as pl
from jax.experimental.pallas import tpu as pltpu
from jax.sharding import PartitionSpec as P

MESH = pl.DeviceIdType.MESH
F32 = jnp.float32
BF16 = jnp.bfloat16
I32 = jnp.int32
NN = (((1,), (0,)), ((), ()))
NT = (((1,), (1,)), ((), ()))

DEV = 128
LEVELS = 7
W = 256
R = 64
LEAF = 12
NCOUP = 4
ROWS = 3072
SEG = 24
HALF = 12
MSG = HALF + 1
SPREAD = 37
EARLY = (1, 1, 24, 64, 100)
PITCH = 16


def mesh_id(device):
    return (lax.shift_right_logical(device, 4), device & 15)


def split(value):
    high = value.astype(BF16)
    return high, (value - high.astype(F32)).astype(BF16)


def pieces(x):
    high, low = split(x)
    return jnp.concatenate([high, low], 0), high


def dot3(x2, xh, weights, dims):
    wh, wl = split(weights)
    n = xh.shape[0]
    both = lax.dot_general(x2, wh, dims, preferred_element_type=F32)
    cross = lax.dot_general(xh, wl, dims, preferred_element_type=F32)
    return both[:n] + both[n:] + cross


def iota(shape, axis):
    return lax.broadcasted_iota(I32, shape, axis)


def within(index, size):
    return jnp.clip(index, 0, size - 1)


def onehot(mask):
    return jnp.where(mask, 1.0, 0.0)


def trailing_zeros(number):
    total = jnp.int32(0)
    for k in range(1, 8):
        total = total + jnp.where((number & ((1 << k) - 1)) == 0, 1, 0)
    return total


def gather_pairs(steps, source, table, second, store):
    left = iota((1, 128), 1) < R

    def step(k, carry):
        for l in range(128):
            a = table[first(k), l]
            b = table[second(k), l]
            store(k, l, jnp.where(left, source[pl.ds(a, 1), :], source[pl.ds(b, 1), :]))
        return carry

    first, second = second
    lax.fori_loop(0, steps, step, 0)


def double_halves(value):
    left = iota(value.shape, value.ndim - 1) < R
    swapped = pltpu.roll(value, R, value.ndim - 1)
    return jnp.where(left, value, swapped), jnp.where(left, swapped, value)


def double_messages(src, dst, n):
    def group(g, carry):
        lo2, hi2 = double_halves(src[pl.ds(g * 8, 8)])
        for i in range(8):
            at = pl.multiple_of((g * 8 + i) * PITCH, PITCH)
            dst[pl.ds(at, n), :] = lo2[i]
            dst[pl.ds(pl.multiple_of(at + DEV * PITCH, PITCH), n), :] = hi2[i]
        return carry

    lax.fori_loop(0, DEV // 8, group, 0)


def kernel(
    rhs_hbm, map_hbm, seprhs_hbm, sepinv_hbm, seppar_hbm, leafinv_hbm, coup_hbm, links,
    came_hbm, pos_hbm, sep_hbm,
    rhs, rmap, seprhs, sepinv, seppar, leafinv, coup,
    doubled, sbuf, rbuf, received, grouped, solved, sbuf2,
    anc, crit, sepout, acc, qt, cums, labels, pos_v, idx_v, idx, idx_r,
    in_sem, loc_sem, crit_send, crit_recv, part_recv, zero_send, zero_recv, five_send, five_recv,
    scat_send, scat_recv, ag_send, ag_recv, a_send, a_recv, b_send, b_recv,
):
    me = lax.axis_index("row") * 16 + lax.axis_index("col")

    loads = [
        pltpu.make_async_copy(s, d, in_sem.at[i])
        for i, (s, d) in enumerate(
            (
                (sepinv_hbm, sepinv), (seprhs_hbm, seprhs), (map_hbm, rmap), (seppar_hbm, seppar),
                (rhs_hbm, rhs), (coup_hbm, coup), (leafinv_hbm, leafinv),
            )
        )
    ]
    for load in loads:
        load.start()

    barrier = pltpu.get_barrier_semaphore()

    def greet(k):
        pl.semaphore_signal(barrier, inc=1, device_id=mesh_id(me ^ k), device_id_type=MESH)

    for k in range(1, 8):
        greet(k)

    def greet8(i, carry):
        for k in range(8):
            greet(i * 8 + k)
        return carry

    lax.fori_loop(1, DEV // 8, greet8, 0)

    own = 6 - trailing_zeros(me + 1)
    reach = lax.shift_right_logical(jnp.int32(32), jnp.clip(own, 0, 5))
    inner = (own >= 0) & (own < 6)
    x_at = me & 3
    even = (me & 1) == 0

    def remote(src, dst, send, recv, to):
        return pltpu.make_async_remote_copy(
            src_ref=src, dst_ref=dst, send_sem=send, recv_sem=recv, device_id=mesh_id(to), device_id_type=MESH
        )

    def rows_of(first, count):
        return anc.at[pl.ds(pl.multiple_of(first, 8), count)]

    def drain(count, sem):
        pltpu.make_async_copy(anc.at[pl.ds(0, count)], anc.at[pl.ds(0, count)], sem).wait()

    def set_level(m, value):
        anc[m * R:(m + 1) * R, :] = value

    def to_children(act):
        @pl.when(inner)
        def _():
            act(remote(sepout, crit, crit_send.at[0], crit_recv, me - reach))
            act(remote(sepout, crit, crit_send.at[1], crit_recv, me + reach))

    def to_partner():
        return remote(sepout, rows_of(6 * R, R), crit_send.at[0], part_recv, me + 1)

    def zero_to(to, which):
        return remote(crit, rows_of(0, R), zero_send.at[which], zero_recv, to)

    def five_to():
        return remote(sepout, rows_of(5 * R, R), five_send, five_recv, me + 2)

    def finish_solve(target):
        t2, th = pieces(target)
        sepout[...] = dot3(t2, th, sepinv[...], NT)

    def take_and_solve():
        pltpu.make_async_copy(sepout, crit, crit_recv).wait()
        p2, ph = pieces(crit[...])
        finish_solve(seprhs[...] - dot3(p2, ph, seppar[...], NN))

    loads[0].wait()
    loads[1].wait()

    @pl.when(own == 0)
    def _():
        finish_solve(seprhs[...])

    @pl.when(own < 0)
    def _():
        sepout[...] = jnp.zeros_like(sepout)

    loads[2].wait()
    rows = rmap[...]
    dest = lax.shift_right_logical(lax.shift_right_logical(rows, 10) * 171, 9)
    local = rows - dest * ROWS
    for j in range(12):
        for h in range(2):
            r = 2 * j + h
            qt[j * 128:(j + 1) * 128, h * 128:(h + 1) * 128] = onehot(
                iota((128, 128), 0) == dest[r:r + 1, :]
            ).astype(BF16)
    tri = onehot((iota((256, 384), 0) < iota((256, 384), 1)) | (iota((256, 384), 1) >= 256)).astype(BF16)
    cums[...] = lax.dot_general(qt[...], tri, NN, preferred_element_type=F32)
    carry = jnp.zeros((128, 128), F32)
    table = jnp.zeros((128, 128), F32)
    sub32 = iota((32, 128), 0)
    lane = iota((1, 128), 1)
    for j in range(12):
        parts = []
        for h in range(2):
            r = 2 * j + h
            q = qt[j * 128:(j + 1) * 128, h * 128:(h + 1) * 128].astype(F32)
            rank = jnp.sum(q * (cums[j * 128:(j + 1) * 128, h * 128:(h + 1) * 128] + carry), axis=0, keepdims=True)
            rank = rank.astype(I32)
            hit = sub32 == rank
            loc = local[r:r + 1, :]
            parts.append(
                jnp.concatenate(
                    [
                        jnp.where(hit, float(r), 0.0),
                        jnp.where(hit, lane.astype(F32), 0.0),
                        jnp.where(hit, lax.shift_right_logical(loc, 7).astype(F32), 0.0),
                        jnp.where(hit, (loc & 127).astype(F32), 0.0),
                    ],
                    0,
                )
            )
            at = dest[r:r + 1, :] * PITCH + rank + jnp.where(rank >= HALF, DEV * PITCH - HALF, 0)
            pos_v[r:r + 1, :] = within(at, 2 * DEV * PITCH)
        digits = jnp.concatenate(parts, 1).astype(BF16)
        table = table + lax.dot_general(digits, qt[j * 128:(j + 1) * 128, :], NT, preferred_element_type=F32)
        carry = carry + cums[j * 128:(j + 1) * 128, 256:384]
    idx_v[0:24, :] = within((table[0:24] * 128.0 + table[32:56]).astype(I32), ROWS)
    to_idx = pltpu.make_async_copy(idx_v.at[pl.ds(0, 24)], idx, loc_sem.at[0])
    to_idx.start()
    to_pos = pltpu.make_async_copy(pos_v, pos_hbm, loc_sem.at[1])
    to_pos.start()
    lab = table[64:96] * 128.0 + table[96:128]
    labels[...] = jnp.concatenate([lab, jnp.zeros((96, 128), F32)], 0).T

    loads[4].wait()

    def double_rhs(j, carry):
        block = rhs[:, pl.ds(pl.multiple_of(j * 128, 128), 128)]
        doubled[pl.ds(pl.multiple_of(j * 128, 128), 128), :] = jnp.concatenate([block, block], 0).T
        return carry

    lax.fori_loop(0, ROWS // 128, double_rhs, 0, unroll=4)

    to_idx.wait()

    def put_send(k, l, row):
        sbuf[l, pl.ds(k, 1), :] = row

    gather_pairs(HALF, doubled, idx, (lambda k: k, lambda k: k + HALF), put_send)
    for l in range(128):
        sbuf[l, HALF:MSG, :] = labels[l:l + 1, :]

    def exchange(src, dst, send, recv, first, last):
        def go(k, carry):
            to = me ^ ((k * SPREAD) & (DEV - 1))
            remote(src.at[to], dst.at[me], send, recv, to).start()
            return carry

        lax.fori_loop(first, last, go, 0)

    def exchange_wait(src, dst, sem):
        n = DEV - 1
        pltpu.make_async_copy(src.at[pl.ds(0, n)], dst.at[pl.ds(0, n)], sem).wait()

    keep = pltpu.make_async_copy(sbuf.at[me], rbuf.at[me], loc_sem.at[2])
    keep.start()
    loads[3].wait()
    pl.semaphore_wait(barrier, DEV - 1)

    @pl.when(own == 0)
    def _():
        to_children(lambda c: c.start())

    @pl.when(own == 1)
    def _():
        take_and_solve()
        to_children(lambda c: c.start())
        zero_to(me - reach, 0).start()
        zero_to(me + reach, 1).start()

    early = jnp.int32(DEV)
    for l, count in enumerate(EARLY):
        early = jnp.where(own == l, count, early)
    exchange(sbuf, rbuf, a_send, a_recv, 1, early)

    @pl.when((own >= 2) & (own <= 4))
    def _():
        take_and_solve()
        to_children(lambda c: c.start())

    @pl.when(own == 2)
    def _():
        set_level(1, crit[...])
        set_level(2, sepout[...])
        drain(R, zero_recv)

        def tile(i, carry):
            to = (me & 96) | (i // 3 * 4 + i % 3)
            remote(rows_of(i * 8, 8), rows_of(i * 8, 8), scat_send, scat_recv.at[0], to).start()
            return carry

        lax.fori_loop(0, 24, tile, 0)

    @pl.when(own == 3)
    def _():
        set_level(3, sepout[...])
        for i in range(8):
            part = rows_of(3 * R + 8 * i, 8)
            remote(part, part, scat_send, scat_recv.at[1], (me & 112) | (i // 2 * 4 + i % 2 * 2)).start()

    @pl.when(own == 4)
    def _():
        set_level(4, sepout[...])
        for i in range(4):
            part = rows_of(4 * R + 16 * i, 16)
            remote(part, part, scat_send, scat_recv.at[2], (me & 120) | (i // 2 * 4 + i % 2 * 2)).start()

    exchange(sbuf, rbuf, a_send, a_recv, early, DEV)

    @pl.when(x_at != 3)
    def _():
        drain(8, scat_recv.at[0])
        part = rows_of((lax.shift_right_logical(me, 2) & 7) * 24 + x_at * 8, 8)

        def hand(k, carry):
            to = me ^ k

            @pl.when((to & 31) != 15)
            def _():
                remote(part, part, ag_send.at[0], ag_recv.at[0], to).start()

            return carry

        lax.fori_loop(1, 32, hand, 0)

    @pl.when(even)
    def _():
        drain(8, scat_recv.at[1])
        part = rows_of(3 * R + (lax.shift_right_logical(me, 2) & 3) * 16 + x_at * 4, 8)

        def hand(k, carry):
            to = me ^ k

            @pl.when((to & 15) != 7)
            def _():
                remote(part, part, ag_send.at[1], ag_recv.at[1], to).start()

            return carry

        lax.fori_loop(1, 16, hand, 0)

    loads[5].wait()
    acc[...] = jnp.zeros_like(acc)

    def level(m, carry):
        p = LEVELS - 1 - m
        x2, xh = pieces(anc[pl.ds(pl.multiple_of(m * R, R), R), :])

        def blocks(g, c0):
            for u in range(4):
                s = g * 4 + u
                which = jnp.int32(0)
                found = jnp.int32(0)
                for c in range(NCOUP):
                    here = jnp.where(links[c, s] == p, 1, 0)
                    which = jnp.where(here > 0, c, which)
                    found = found + here
                term = dot3(x2, xh, coup[s * NCOUP + which], NN)
                acc[s] += jnp.where(found > 0, term, 0.0)
            return c0

        lax.fori_loop(0, LEAF // 4, blocks, 0)
        return carry

    @pl.when((x_at != 3))
    def _():
        drain(184, ag_recv.at[0])

    @pl.when((x_at == 3) & (own != 2))
    def _():
        drain(192, ag_recv.at[0])

    lax.fori_loop(0, 3, level, 0)

    @pl.when(own == 5)
    def _():
        take_and_solve()
        to_children(lambda c: c.start())
        five_to().start()
        set_level(4, crit[...])
        set_level(5, sepout[...])

    @pl.when(even)
    def _():
        drain(16, scat_recv.at[2])
        part = rows_of(4 * R + (lax.shift_right_logical(me, 2) & 1) * 32 + x_at * 8, 16)
        for low in (0, 2, 4, 6, 7):
            @pl.when((me & 7) != low)
            def _():
                remote(part, part, ag_send.at[2], ag_recv.at[2], (me & 120) | low).start()

    exchange_wait(sbuf, rbuf, a_recv)
    keep.wait()
    for p in range(128):
        labels[p:p + 1, :] = rbuf[p, HALF:MSG, :]
    got = labels[...].T[0:32].astype(I32)
    high = lax.shift_right_logical(got, 7)
    low = got & 127
    inverse = jnp.zeros((64, 128), F32)
    for j in range(12):
        aa, bb = [], []
        for h in range(2):
            r = 2 * j + h
            at = lane * PITCH + (r % HALF + (r // HALF) * DEV * PITCH)
            hit = sub32 == high[r:r + 1, :]
            aa.append(
                jnp.concatenate(
                    [
                        jnp.where(hit, lax.shift_right_logical(at, 6).astype(F32), 0.0),
                        jnp.where(hit, (at & 63).astype(F32), 0.0),
                    ],
                    0,
                )
            )
            bb.append(onehot(iota((128, 128), 0) == low[r:r + 1, :]))
        inverse = inverse + lax.dot_general(
            jnp.concatenate(aa, 1).astype(BF16), jnp.concatenate(bb, 1).astype(BF16), NT, preferred_element_type=F32
        )
    idx_v[0:24, :] = within((inverse[0:24] * 64.0 + inverse[32:56]).astype(I32), 2 * DEV * PITCH)
    idx_v[24:48, :] = within(((high & 1) * (ROWS // 2) + lax.shift_right_logical(high, 1) * 128 + low)[0:24], ROWS)
    to_idx = pltpu.make_async_copy(idx_v, idx_r, loc_sem.at[0])
    to_idx.start()

    double_messages(rbuf, received, MSG)
    to_idx.wait()

    def put_grouped(k, l, row):
        grouped[pl.ds(k * 128 + l, 1), :] = row

    gather_pairs(LEAF, received, idx_r, (lambda k: 2 * k, lambda k: 2 * k + 1), put_grouped)

    @pl.when(own == 6)
    def _():
        take_and_solve()
        to_partner().start()
        set_level(5, crit[...])
        set_level(6, sepout[...])

    @pl.when(even)
    def _():
        drain(56, ag_recv.at[1])
        drain(48, ag_recv.at[2])

    @pl.when(~even & ((me & 15) != 7))
    def _():
        drain(64, ag_recv.at[1])

    @pl.when((me & 7) == 7)
    def _():
        drain(64, ag_recv.at[2])

    lax.fori_loop(3, 5, level, 0)

    @pl.when(x_at == 3)
    def _():
        drain(R, five_recv)

    lax.fori_loop(5, 6, level, 0)

    @pl.when(~even)
    def _():
        drain(R, part_recv)

    lax.fori_loop(6, 7, level, 0)

    loads[6].wait()

    def leaf(g, carry):
        for u in range(4):
            t = g * 4 + u
            at = pl.multiple_of(t * 128, 128)
            both = grouped[pl.ds(at, 128), :].T
            target = jnp.concatenate([both[:R], both[R:]], 1) - acc[t]
            t2, th = pieces(target)
            x = dot3(t2, th, leafinv[t], NT)
            solved[pl.ds(at, 128), :] = jnp.concatenate([x[:, :128], x[:, :128]], 0).T
            solved[pl.ds(pl.multiple_of(at + ROWS // 2, 128), 128), :] = jnp.concatenate([x[:, 128:], x[:, 128:]], 0).T
        return carry

    lax.fori_loop(0, LEAF // 4, leaf, 0)

    def put_back(k, l, row):
        sbuf2[l, pl.ds(k, 1), :] = row

    gather_pairs(HALF, solved, idx_r, (lambda k: k + 24, lambda k: k + 24 + HALF), put_back)
    mine = pltpu.make_async_copy(sbuf2.at[me], came_hbm.at[me], loc_sem.at[2])
    mine.start()
    exchange(sbuf2, came_hbm, b_send, b_recv, 1, DEV)
    out_sep = pltpu.make_async_copy(sepout, sep_hbm, loc_sem.at[3])
    out_sep.start()

    exchange_wait(sbuf, rbuf, a_send)
    to_children(lambda c: c.wait_send())

    @pl.when(own == 6)
    def _():
        to_partner().wait_send()

    @pl.when(own == 5)
    def _():
        five_to().wait_send()

    @pl.when(own == 1)
    def _():
        zero_to(me - reach, 0).wait_send()
        zero_to(me + reach, 1).wait_send()

    @pl.when(own == 2)
    def _():
        drain(192, scat_send)

    @pl.when((own == 3) | (own == 4))
    def _():
        drain(64, scat_send)

    @pl.when(x_at != 3)
    def _():
        drain(240, ag_send.at[0])

    @pl.when(even)
    def _():
        drain(112, ag_send.at[1])
        drain(64, ag_send.at[2])

    to_pos.wait()
    out_sep.wait()
    mine.wait()
    exchange_wait(sbuf2, came_hbm, b_recv)
    exchange_wait(sbuf2, came_hbm, b_send)


def restore_kernel(came_hbm, pos, sep_hbm, x_hbm, sepx_hbm, came, returned, grouped, xout, sem, out_sem):
    load = pltpu.make_async_copy(came_hbm, came, sem.at[0])
    load.start()
    move = pltpu.make_async_copy(sep_hbm, sepx_hbm, sem.at[1])
    move.start()
    load.wait()
    double_messages(came, returned, HALF)
    left = iota((1, 128), 1) < R

    def put(j):
        return pltpu.make_async_copy(
            xout.at[:, pl.ds(pl.multiple_of(j * 256, 256), 256)],
            x_hbm.at[:, pl.ds(pl.multiple_of(j * 256, 256), 256)],
            out_sem,
        )

    def restore(j, carry):
        for l in range(128):
            a = pos[2 * j, l]
            b = pos[2 * j + 1, l]
            grouped[pl.ds(j * 128 + l, 1), :] = jnp.where(left, returned[pl.ds(a, 1), :], returned[pl.ds(b, 1), :])
        both = grouped[pl.ds(pl.multiple_of(j * 128, 128), 128), :].T
        xout[:, pl.ds(pl.multiple_of(j * 256, 256), 256)] = jnp.concatenate([both[:R], both[R:]], 1)
        put(j).start()
        return carry

    lax.fori_loop(0, LEAF, restore, 0)
    pltpu.make_async_copy(xout, x_hbm, out_sem).wait()
    move.wait()


def per_device(rhs_held, row_map, sep_rhs, sep_inverse, sep_parent, leaf_inverse, leaf_coupling, leaf_links):
    hbm = pl.BlockSpec(memory_space=pltpu.HBM)
    vmem = pltpu.VMEM
    came, pos, sep = pl.pallas_call(
        kernel,
        out_shape=(
            jax.ShapeDtypeStruct((DEV, HALF, 128), F32),
            jax.ShapeDtypeStruct((24, 128), I32),
            jax.ShapeDtypeStruct((R, W), F32),
        ),
        in_specs=[hbm] * 7 + [pl.BlockSpec(memory_space=pltpu.SMEM)],
        out_specs=(hbm, hbm, hbm),
        scratch_shapes=[
            vmem((R, ROWS), F32),
            vmem((24, 128), I32),
            vmem((R, W), F32),
            vmem((W, W), F32),
            vmem((W, W), F32),
            vmem((LEAF, W, W), F32),
            vmem((LEAF * NCOUP, W, W), F32),
            vmem((ROWS, 128), F32),
            vmem((DEV, MSG, 128), F32),
            vmem((DEV, MSG, 128), F32),
            vmem((2 * DEV * PITCH, 128), F32),
            vmem((ROWS // 2, 128), F32),
            vmem((ROWS, 128), F32),
            vmem((DEV, HALF, 128), F32),
            vmem((LEVELS * R, W), F32),
            vmem((R, W), F32),
            vmem((R, W), F32),
            vmem((LEAF, R, W), F32),
            vmem((12 * 128, 256), BF16),
            vmem((12 * 128, 384), F32),
            vmem((128, 128), F32),
            vmem((24, 128), I32),
            vmem((48, 128), I32),
            pltpu.SMEM((24, 128), I32),
            pltpu.SMEM((48, 128), I32),
            pltpu.SemaphoreType.DMA((7,)),
            pltpu.SemaphoreType.DMA((4,)),
            pltpu.SemaphoreType.DMA((2,)),
            pltpu.SemaphoreType.DMA,
            pltpu.SemaphoreType.DMA,
            pltpu.SemaphoreType.DMA((2,)),
            pltpu.SemaphoreType.DMA,
            pltpu.SemaphoreType.DMA,
            pltpu.SemaphoreType.DMA,
            pltpu.SemaphoreType.DMA,
            pltpu.SemaphoreType.DMA((3,)),
            pltpu.SemaphoreType.DMA((3,)),
            pltpu.SemaphoreType.DMA((3,)),
            pltpu.SemaphoreType.DMA,
            pltpu.SemaphoreType.DMA,
            pltpu.SemaphoreType.DMA,
            pltpu.SemaphoreType.DMA,
        ],
        compiler_params=pltpu.CompilerParams(
            collective_id=0, has_side_effects=True, vmem_limit_bytes=56 << 20
        ),
        name="gmrf_solve",
    )(
        rhs_held.T,
        row_map.reshape(24, 128),
        sep_rhs[0].T,
        sep_inverse[0],
        sep_parent[0],
        leaf_inverse[0],
        leaf_coupling[0].reshape(LEAF * NCOUP, W, W),
        leaf_links[0].T,
    )
    x, sep = pl.pallas_call(
        restore_kernel,
        out_shape=(jax.ShapeDtypeStruct((R, ROWS), F32), jax.ShapeDtypeStruct((R, W), F32)),
        in_specs=[hbm, pl.BlockSpec(memory_space=pltpu.SMEM), hbm],
        out_specs=(hbm, hbm),
        scratch_shapes=[
            vmem((DEV, HALF, 128), F32),
            vmem((2 * DEV * PITCH, 128), F32),
            vmem((ROWS // 2, 128), F32),
            vmem((R, ROWS), F32),
            pltpu.SemaphoreType.DMA((2,)),
            pltpu.SemaphoreType.DMA,
        ],
        compiler_params=pltpu.CompilerParams(vmem_limit_bytes=56 << 20),
        name="restore_rows",
    )(came, pos, sep)
    return x.T, sep.T[None]


def solution(mesh):
    in_specs = (
        P(("row", "col"), None),
        P(("row", "col")),
        P(("row", "col"), None, None),
        P(("row", "col"), None, None),
        P(("row", "col"), None, None),
        P(("row", "col"), None, None, None),
        P(("row", "col"), None, None, None, None),
        P(("row", "col"), None, None),
    )
    out_specs = (P(("row", "col"), None), P(("row", "col"), None, None))
    return jax.shard_map(per_device, mesh=mesh, in_specs=in_specs, out_specs=out_specs, check_vma=False)
```

```python
import functools

import jax
import jax.numpy as jnp
from jax import lax
from jax.experimental import pallas as pl
from jax.experimental.pallas import tpu as pltpu
from jax.sharding import PartitionSpec as P

MESH = pl.DeviceIdType.MESH
F32 = jnp.float32
BF16 = jnp.bfloat16
I32 = jnp.int32
NN = (((1,), (0,)), ((), ()))
NT = (((1,), (1,)), ((), ()))

DEV = 128
LEVELS = 7
W = 256
R = 64
LEAF = 12
NCOUP = 4
ROWS = 3072
SEG = 24
HALF = 12
MSG = HALF + 1
SPREAD = 11
CUTS = 4
PITCH = 16


def mesh_id(device):
    return (lax.shift_right_logical(device, 4), device & 15)


def split(value):
    high = value.astype(BF16)
    return high, (value - high.astype(F32)).astype(BF16)


def pieces(x):
    high, low = split(x)
    return jnp.concatenate([high, low], 0), high


def dot3(x2, xh, weights, dims):
    wh, wl = split(weights)
    n = xh.shape[0]
    both = lax.dot_general(x2, wh, dims, preferred_element_type=F32)
    cross = lax.dot_general(xh, wl, dims, preferred_element_type=F32)
    return both[:n] + both[n:] + cross


def iota(shape, axis):
    return lax.broadcasted_iota(I32, shape, axis)


def within(index, size):
    return jnp.clip(index, 0, size - 1)


def onehot(mask):
    return jnp.where(mask, 1.0, 0.0)


def trailing_zeros(number):
    total = jnp.int32(0)
    for k in range(1, 8):
        total = total + jnp.where((number & ((1 << k) - 1)) == 0, 1, 0)
    return total


def gather_pairs(steps, source, table, first, second, store, lanes=range(128)):
    left = iota((1, 128), 1) < R

    def step(k, carry):
        for l in lanes:
            a = table[first(k), l]
            b = table[second(k), l]
            store(k, l, jnp.where(left, source[pl.ds(a, 1), :], source[pl.ds(b, 1), :]))
        return carry

    lax.fori_loop(0, steps, step, 0)


def swap_halves(both, first=0, count=DEV * PITCH):
    def group(g, carry):
        at = pl.multiple_of(first + g * 128, 128)
        both[pl.ds(at + DEV * PITCH, 128), :] = pltpu.roll(both[pl.ds(at, 128), :], R, 1)
        return carry

    lax.fori_loop(0, count // 128, group, 0, unroll=2)


def kernel(
    rhs_hbm, map_hbm, seprhs_hbm, sepinv_hbm, seppar_hbm, leafinv_hbm, coup_hbm, links,
    came_hbm, pos_hbm, sep_hbm,
    rhs, rmap, seprhs, sepinv, seppar, leafinv, coup,
    doubled, sbuf, received, grouped, solved, sbuf2,
    anc, crit, sepout, ready, acc, qt, cums, labels, pos_v, idx_v, idx, idx_r,
    in_sem, loc_sem, crit_send, crit_recv, part_recv, zero_send, zero_recv, four_send, four_recv, five_send, five_recv,
    scat_send, scat_recv, ag_send, ag_recv, a_send, a_recv, b_send, b_recv, gate,
):
    me = lax.axis_index("row") * 16 + lax.axis_index("col")

    loads = [
        pltpu.make_async_copy(s, d, in_sem.at[i])
        for i, (s, d) in enumerate(
            (
                (sepinv_hbm, sepinv), (seprhs_hbm, seprhs), (map_hbm, rmap), (seppar_hbm, seppar),
                (rhs_hbm, rhs), (coup_hbm, coup), (leafinv_hbm, leafinv),
            )
        )
    ]
    for load in loads:
        load.start()

    barrier = pltpu.get_barrier_semaphore()

    for k in [16 * i for i in range(1, 8)] + list(range(1, 16)):
        pl.semaphore_signal(barrier, inc=1, device_id=mesh_id(me ^ k), device_id_type=MESH)

    own = 6 - trailing_zeros(me + 1)
    reach = lax.shift_right_logical(jnp.int32(32), jnp.clip(own, 0, 5))
    inner = (own >= 0) & (own < 6)
    x_at = me & 3
    even = (me & 1) == 0

    def remote(src, dst, send, recv, to):
        return pltpu.make_async_remote_copy(
            src_ref=src, dst_ref=dst, send_sem=send, recv_sem=recv, device_id=mesh_id(to), device_id_type=MESH
        )

    def rows_of(first, count):
        return anc.at[pl.ds(pl.multiple_of(first, 8), count)]

    def drain(count, sem):
        pltpu.make_async_copy(anc.at[pl.ds(0, count)], anc.at[pl.ds(0, count)], sem).wait()

    def set_level(m, value):
        anc[m * R:(m + 1) * R, :] = value

    def to_children(act, cuts):
        @pl.when(inner)
        def _():
            for i in range(cuts):
                part = pl.ds(i * (R // cuts), R // cuts)
                act(remote(sepout.at[part], crit.at[part], crit_send.at[0], crit_recv, me - reach))
                act(remote(sepout.at[part], crit.at[part], crit_send.at[1], crit_recv, me + reach))

    def start_children():
        to_children(lambda c: c.start(), CUTS)

    def finish_children():
        to_children(lambda c: c.wait_send(), 1)

    def to_partner():
        return remote(sepout, rows_of(6 * R, R), crit_send.at[0], part_recv, me + 1)

    def zero_to(to, which):
        return remote(crit, rows_of(0, R), zero_send.at[which], zero_recv, to)

    def four_to():
        return [
            remote(sepout, rows_of(4 * R, R), four_send.at[i], four_recv, (me & 120) | low)
            for i, low in enumerate((0, 2, 7, 4, 6))
        ]

    def five_to():
        return remote(crit, rows_of(5 * R, R), five_send, five_recv, me + 3)

    def finish_solve(target):
        t2, th = pieces(target)
        sepout[...] = dot3(t2, th, sepinv[...], NT)

    def take_and_solve():
        with jax.named_scope("parent_wait"):
            pltpu.make_async_copy(sepout, crit, crit_recv).wait()

        @pl.when((own == 6) & (x_at == 0))
        def _():
            five_to().start()

        with jax.named_scope("own_solve"):
            p2, ph = pieces(crit[...])
            finish_solve(seprhs[...] - dot3(p2, ph, seppar[...], NN))

    loads[0].wait()
    loads[1].wait()

    @pl.when(own == 0)
    def _():
        finish_solve(seprhs[...])

    pl.semaphore_wait(barrier, 22)

    for i in range(1, 8):
        pl.semaphore_signal(gate, inc=1, device_id=mesh_id(me ^ (16 * i)), device_id_type=MESH)

    @pl.when(own == 0)
    def _():
        start_children()

    @pl.when(own < 0)
    def _():
        sepout[...] = jnp.zeros_like(sepout)

    loads[2].wait()
    rows = rmap[...]
    dest = lax.shift_right_logical(lax.shift_right_logical(rows, 10) * 171, 9)
    local = rows - dest * ROWS
    for j in range(12):
        for h in range(2):
            r = 2 * j + h
            qt[j * 128:(j + 1) * 128, h * 128:(h + 1) * 128] = onehot(
                iota((128, 128), 0) == dest[r:r + 1, :]
            ).astype(BF16)
    tri = onehot((iota((256, 384), 0) < iota((256, 384), 1)) | (iota((256, 384), 1) >= 256)).astype(BF16)
    cums[...] = lax.dot_general(qt[...], tri, NN, preferred_element_type=F32)
    carry = jnp.zeros((128, 128), F32)
    table = jnp.zeros((128, 128), F32)
    sub32 = iota((32, 128), 0)
    lane = iota((1, 128), 1)
    for j in range(12):
        parts = []
        for h in range(2):
            r = 2 * j + h
            q = qt[j * 128:(j + 1) * 128, h * 128:(h + 1) * 128].astype(F32)
            rank = jnp.sum(q * (cums[j * 128:(j + 1) * 128, h * 128:(h + 1) * 128] + carry), axis=0, keepdims=True)
            rank = rank.astype(I32)
            hit = sub32 == rank
            loc = local[r:r + 1, :]
            parts.append(
                jnp.concatenate(
                    [
                        jnp.where(hit, float(r), 0.0),
                        jnp.where(hit, lane.astype(F32), 0.0),
                        jnp.where(hit, lax.shift_right_logical(loc, 7).astype(F32), 0.0),
                        jnp.where(hit, (loc & 127).astype(F32), 0.0),
                    ],
                    0,
                )
            )
            at = dest[r:r + 1, :] * PITCH + rank + jnp.where(rank >= HALF, DEV * PITCH - HALF, 0)
            pos_v[r:r + 1, :] = within(at, 2 * DEV * PITCH) ^ (h * DEV * PITCH)
        digits = jnp.concatenate(parts, 1).astype(BF16)
        table = table + lax.dot_general(digits, qt[j * 128:(j + 1) * 128, :], NT, preferred_element_type=F32)
        carry = carry + cums[j * 128:(j + 1) * 128, 256:384]
    idx_v[0:24, :] = within((table[0:24] * 128.0 + table[32:56]).astype(I32), ROWS)
    to_idx = pltpu.make_async_copy(idx_v.at[pl.ds(0, 24)], idx, loc_sem.at[0])
    to_idx.start()
    to_pos = pltpu.make_async_copy(pos_v, pos_hbm, loc_sem.at[1])
    to_pos.start()
    lab = table[64:96] * 128.0 + table[96:128]
    labels[...] = jnp.concatenate([lab, jnp.zeros((96, 128), F32)], 0).T

    loads[4].wait()

    def double_rhs(j, carry):
        block = rhs[:, pl.ds(pl.multiple_of(j * 128, 128), 128)]
        doubled[pl.ds(pl.multiple_of(j * 128, 128), 128), :] = jnp.concatenate([block, block], 0).T
        return carry

    lax.fori_loop(0, ROWS // 128, double_rhs, 0, unroll=4)

    to_idx.wait()

    def put_send(k, l, row):
        sbuf[pl.ds(l * PITCH + k, 1), :] = row

    def landing(dst, device, n):
        return dst.at[pl.ds(pl.multiple_of(device * PITCH, PITCH), n)]

    def exchange(core, src, dst, n, send, recv):
        def go(k, carry):
            j = (k * SPREAD) & 63
            to = (me ^ ((j & 15) + (j // 16) * 32)) & 111 | (core * 16)

            @pl.when(to != me)
            def _():
                remote(landing(src, to, n), landing(dst, me, n), send, recv, to).start()

            return carry

        lax.fori_loop(0, 64, go, 0)

    def lanes_of(core):
        return [l for l in range(DEV) if (l >> 4) & 1 == core]

    def exchange_wait(rows, n, sem):
        count = (DEV - 1) * n
        pltpu.make_async_copy(rows.at[pl.ds(0, count)], rows.at[pl.ds(0, count)], sem).wait()

    loads[3].wait()

    pl.semaphore_wait(gate, 7)

    @pl.when(own == 0)
    def _():
        finish_children()

    @pl.when((own >= 1) & (own <= 2))
    def _():
        take_and_solve()
        start_children()

    @pl.when(own == 1)
    def _():
        finish_children()
        zero_to(me - reach, 0).start()
        zero_to(me + reach, 1).start()
        zero_to(me - reach, 0).wait_send()
        zero_to(me + reach, 1).wait_send()

    @pl.when(own == 2)
    def _():
        set_level(1, crit[...])
        set_level(2, sepout[...])
        drain(R, zero_recv)

        def tile(i, carry):
            to = (me & 96) | (i // 3 * 4 + i % 3)
            remote(rows_of(i * 8, 8), rows_of(i * 8, 8), scat_send, scat_recv.at[0], to).start()
            return carry

        lax.fori_loop(0, 24, tile, 0)

    gather_pairs(HALF, doubled, idx, lambda k: k, lambda k: k + HALF, put_send)
    for l in range(DEV):
        sbuf[l * PITCH + HALF:l * PITCH + MSG, :] = labels[l:l + 1, :]
    for core in range(2):
        exchange(core, sbuf, received, MSG, a_send, a_recv)
    keep = pltpu.make_async_copy(landing(sbuf, me, MSG), landing(received, me, MSG), loc_sem.at[2])
    keep.start()

    @pl.when(own == 3)
    def _():
        take_and_solve()
        start_children()
        set_level(3, sepout[...])
        for i in range(8):
            part = rows_of(3 * R + 8 * i, 8)
            remote(part, part, scat_send, scat_recv.at[1], (me & 112) | (i // 2 * 4 + i % 2 * 2)).start()

    @pl.when(own == 4)
    def _():
        take_and_solve()
        start_children()
        set_level(4, sepout[...])
        finish_children()
        for c in four_to():
            c.start()

    @pl.when(x_at != 3)
    def _():
        drain(8, scat_recv.at[0])
        part = rows_of((lax.shift_right_logical(me, 2) & 7) * 24 + x_at * 8, 8)

        def hand(k, carry):
            to = me ^ k

            @pl.when((to & 31) != 15)
            def _():
                remote(part, part, ag_send.at[0], ag_recv.at[0], to).start()

            return carry

        lax.fori_loop(1, 32, hand, 0)

    @pl.when(even)
    def _():
        drain(8, scat_recv.at[1])
        part = rows_of(3 * R + (lax.shift_right_logical(me, 2) & 3) * 16 + x_at * 4, 8)

        def hand(k, carry):
            to = me ^ k

            @pl.when((to & 15) != 7)
            def _():
                remote(part, part, ag_send.at[1], ag_recv.at[1], to).start()

            return carry

        lax.fori_loop(1, 16, hand, 0)

    exchange_wait(doubled, MSG, a_recv)
    keep.wait()
    for p in range(128):
        labels[p:p + 1, :] = received[p * PITCH + HALF:p * PITCH + MSG, :]
    got = labels[...].T[0:32].astype(I32)
    high = lax.shift_right_logical(got, 7)
    low = got & 127
    inverse = jnp.zeros((64, 128), F32)
    for j in range(12):
        aa, bb = [], []
        for h in range(2):
            r = 2 * j + h
            at = lane * PITCH + (r % HALF + (r // HALF) * DEV * PITCH)
            hit = sub32 == high[r:r + 1, :]
            aa.append(
                jnp.concatenate(
                    [
                        jnp.where(hit, lax.shift_right_logical(at, 6).astype(F32), 0.0),
                        jnp.where(hit, (at & 63).astype(F32), 0.0),
                    ],
                    0,
                )
            )
            bb.append(onehot(iota((128, 128), 0) == low[r:r + 1, :]))
        inverse = inverse + lax.dot_general(
            jnp.concatenate(aa, 1).astype(BF16), jnp.concatenate(bb, 1).astype(BF16), NT, preferred_element_type=F32
        )
    found_at = within((inverse[0:24] * 64.0 + inverse[32:56]).astype(I32), 2 * DEV * PITCH)
    idx_v[0:24, :] = found_at ^ ((iota((24, 128), 0) & 1) * (DEV * PITCH))
    idx_v[24:48, :] = within(((high & 1) * (ROWS // 2) + lax.shift_right_logical(high, 1) * 128 + low)[0:24], ROWS)
    to_idx = pltpu.make_async_copy(idx_v, idx_r, loc_sem.at[0])
    to_idx.start()

    swap_halves(received)
    @pl.when(own == 5)
    def _():
        take_and_solve()
        start_children()
        set_level(4, crit[...])
        set_level(5, sepout[...])
        finish_children()

    to_idx.wait()

    def put_grouped(k, l, row):
        grouped[pl.ds(k * 128 + l, 1), :] = row

    gather_pairs(LEAF, received, idx_r, lambda k: 2 * k, lambda k: 2 * k + 1, put_grouped)

    @pl.when(own == 6)
    def _():
        take_and_solve()
        to_partner().start()
        set_level(5, crit[...])
        set_level(6, sepout[...])

    loads[5].wait()

    def make_ready(m):
        x2, _ = pieces(anc[m * R:(m + 1) * R, :])
        ready[m] = x2

    def block(i):
        def blocks(g, carry):
            for u in range(4):
                s = g * 4 + u
                link = [links[c, s] for c in range(NCOUP)]
                which = jnp.int32(0)
                level = jnp.int32(0)
                for c in range(NCOUP):
                    above = jnp.int32(0)
                    for other in range(NCOUP):
                        if other != c:
                            above = above + jnp.where(link[other] > link[c], 1, 0)
                    which = jnp.where(above == i, c, which)
                    level = jnp.where(above == i, LEVELS - 1 - link[c], level)
                x2 = ready[level]
                term = dot3(x2, x2[:R], coup[s * NCOUP + which], NN)
                acc[s] = term if i == 0 else acc[s] + term
            return carry

        lax.fori_loop(0, LEAF // 4, blocks, 0)

    @pl.when((x_at != 3))
    def _():
        drain(184, ag_recv.at[0])

    @pl.when((x_at == 3) & (own != 2))
    def _():
        drain(192, ag_recv.at[0])

    @pl.when(even)
    def _():
        drain(56, ag_recv.at[1])

    @pl.when(~even & ((me & 15) != 7))
    def _():
        drain(64, ag_recv.at[1])

    for m in range(4):
        make_ready(m)
    block(0)

    @pl.when(even | ((me & 7) == 7))
    def _():
        drain(R, four_recv)

    make_ready(4)
    block(1)

    @pl.when(x_at == 3)
    def _():
        drain(R, five_recv)

    make_ready(5)
    block(2)

    @pl.when(~even)
    def _():
        drain(R, part_recv)

    make_ready(6)
    block(3)

    loads[6].wait()

    def leaf(g, carry):
        for u in range(4):
            t = g * 4 + u
            at = pl.multiple_of(t * 128, 128)
            both = grouped[pl.ds(at, 128), :].T
            target = jnp.concatenate([both[:R], both[R:]], 1) - acc[t]
            t2, th = pieces(target)
            x = dot3(t2, th, leafinv[t], NT)
            solved[pl.ds(at, 128), :] = jnp.concatenate([x[:, :128], x[:, :128]], 0).T
            solved[pl.ds(pl.multiple_of(at + ROWS // 2, 128), 128), :] = jnp.concatenate([x[:, 128:], x[:, 128:]], 0).T
        return carry

    lax.fori_loop(0, LEAF // 4, leaf, 0)

    def put_back(k, l, row):
        sbuf2[pl.ds(l * PITCH + k, 1), :] = row

    for core in range(2):
        gather_pairs(HALF, solved, idx_r, lambda k: k + 24, lambda k: k + 24 + HALF, put_back, lanes_of(core))
        exchange(core, sbuf2, came_hbm, HALF, b_send, b_recv)
    mine = pltpu.make_async_copy(landing(sbuf2, me, HALF), landing(came_hbm, me, HALF), loc_sem.at[2])
    mine.start()
    out_sep = pltpu.make_async_copy(sepout, sep_hbm, loc_sem.at[3])
    out_sep.start()

    exchange_wait(doubled, MSG, a_send)

    @pl.when(own == 6)
    def _():
        to_partner().wait_send()

    @pl.when(x_at == 0)
    def _():
        five_to().wait_send()

    @pl.when((own == 2) | (own == 3))
    def _():
        finish_children()

    @pl.when(own == 2)
    def _():
        drain(192, scat_send)

    @pl.when(own == 3)
    def _():
        drain(64, scat_send)

    @pl.when(own == 4)
    def _():
        for c in four_to():
            c.wait_send()

    @pl.when(x_at != 3)
    def _():
        drain(240, ag_send.at[0])

    @pl.when(even)
    def _():
        drain(112, ag_send.at[1])

    to_pos.wait()
    out_sep.wait()
    mine.wait()
    exchange_wait(doubled, HALF, b_recv)
    exchange_wait(doubled, HALF, b_send)


def restore_kernel(came_hbm, pos, sep_hbm, x_hbm, sepx_hbm, came, grouped, xout, sem, out_sem):
    part = DEV * PITCH // 4
    loads = [
        pltpu.make_async_copy(came_hbm.at[pl.ds(i * part, part)], came.at[pl.ds(i * part, part)], sem.at[2 + i])
        for i in range(4)
    ]
    for load in loads:
        load.start()
    move = pltpu.make_async_copy(sep_hbm, sepx_hbm, sem.at[1])
    move.start()
    with jax.named_scope("load_and_swap"):
        for i in range(4):
            loads[i].wait()
            swap_halves(came, i * part, part)
    left = iota((1, 128), 1) < R

    def pick(j, slot):
        for l in range(128):
            a = pos[2 * j, l]
            b = pos[2 * j + 1, l]
            grouped[slot, l:l + 1, :] = jnp.where(left, came[pl.ds(a, 1), :], came[pl.ds(b, 1), :])

    def write(j, slot):
        at = pl.ds(pl.multiple_of(j * 256, 256), 256)
        both = grouped[slot].T
        xout[:, at] = jnp.concatenate([both[:R], both[R:]], 1)
        pltpu.make_async_copy(xout.at[:, at], x_hbm.at[:, at], out_sem).start()

    with jax.named_scope("pick_first"):
        pick(0, 0)

    def step(i, carry):
        j = 2 * i
        pick(j + 1, 1)
        write(j, 0)
        pick(jnp.minimum(j + 2, LEAF - 1), 0)
        write(j + 1, 1)
        return carry

    with jax.named_scope("pick_and_write"):
        lax.fori_loop(0, LEAF // 2, step, 0)
    with jax.named_scope("drain"):
        pltpu.make_async_copy(xout, x_hbm, out_sem).wait()
        move.wait()


def per_device(rhs_held, row_map, sep_rhs, sep_inverse, sep_parent, leaf_inverse, leaf_coupling, leaf_links):
    hbm = pl.BlockSpec(memory_space=pltpu.HBM)
    vmem = pltpu.VMEM
    came, pos, sep = pl.pallas_call(
        kernel,
        out_shape=(
            jax.ShapeDtypeStruct((DEV * PITCH, 128), F32),
            jax.ShapeDtypeStruct((24, 128), I32),
            jax.ShapeDtypeStruct((R, W), F32),
        ),
        in_specs=[hbm] * 7 + [pl.BlockSpec(memory_space=pltpu.SMEM)],
        out_specs=(hbm, hbm, hbm),
        scratch_shapes=[
            vmem((R, ROWS), F32),
            vmem((24, 128), I32),
            vmem((R, W), F32),
            vmem((W, W), F32),
            vmem((W, W), F32),
            vmem((LEAF, W, W), F32),
            vmem((LEAF * NCOUP, W, W), F32),
            vmem((ROWS, 128), F32),
            vmem((DEV * PITCH, 128), F32),
            vmem((2 * DEV * PITCH, 128), F32),
            vmem((ROWS // 2, 128), F32),
            vmem((ROWS, 128), F32),
            vmem((DEV * PITCH, 128), F32),
            vmem((LEVELS * R, W), F32),
            vmem((R, W), F32),
            vmem((R, W), F32),
            vmem((LEVELS, 2 * R, W), BF16),
            vmem((LEAF, R, W), F32),
            vmem((12 * 128, 256), BF16),
            vmem((12 * 128, 384), F32),
            vmem((128, 128), F32),
            vmem((24, 128), I32),
            vmem((48, 128), I32),
            pltpu.SMEM((24, 128), I32),
            pltpu.SMEM((48, 128), I32),
            pltpu.SemaphoreType.DMA((7,)),
            pltpu.SemaphoreType.DMA((4,)),
            pltpu.SemaphoreType.DMA((2,)),
            pltpu.SemaphoreType.DMA,
            pltpu.SemaphoreType.DMA,
            pltpu.SemaphoreType.DMA((2,)),
            pltpu.SemaphoreType.DMA,
            pltpu.SemaphoreType.DMA((5,)),
            pltpu.SemaphoreType.DMA,
            pltpu.SemaphoreType.DMA,
            pltpu.SemaphoreType.DMA,
            pltpu.SemaphoreType.DMA,
            pltpu.SemaphoreType.DMA((2,)),
            pltpu.SemaphoreType.DMA((2,)),
            pltpu.SemaphoreType.DMA((2,)),
            pltpu.SemaphoreType.DMA,
            pltpu.SemaphoreType.DMA,
            pltpu.SemaphoreType.DMA,
            pltpu.SemaphoreType.DMA,
            pltpu.SemaphoreType.REGULAR,
        ],
        compiler_params=pltpu.CompilerParams(
            collective_id=0, has_side_effects=True, vmem_limit_bytes=56 << 20
        ),
        name="gmrf_solve",
    )(
        rhs_held.T,
        row_map.reshape(24, 128),
        sep_rhs[0].T,
        sep_inverse[0],
        sep_parent[0],
        leaf_inverse[0],
        leaf_coupling[0].reshape(LEAF * NCOUP, W, W),
        leaf_links[0].T,
    )
    x, sep = pl.pallas_call(
        restore_kernel,
        out_shape=(jax.ShapeDtypeStruct((R, ROWS), F32), jax.ShapeDtypeStruct((R, W), F32)),
        in_specs=[hbm, pl.BlockSpec(memory_space=pltpu.SMEM), hbm],
        out_specs=(hbm, hbm),
        scratch_shapes=[
            vmem((2 * DEV * PITCH, 128), F32),
            vmem((2, 128, 128), F32),
            vmem((R, ROWS), F32),
            pltpu.SemaphoreType.DMA((6,)),
            pltpu.SemaphoreType.DMA,
        ],
        compiler_params=pltpu.CompilerParams(vmem_limit_bytes=56 << 20),
        name="restore_rows",
    )(came, pos, sep)
    return x.T, sep.T[None]


def solution(mesh):
    in_specs = (
        P(("row", "col"), None),
        P(("row", "col")),
        P(("row", "col"), None, None),
        P(("row", "col"), None, None),
        P(("row", "col"), None, None),
        P(("row", "col"), None, None, None),
        P(("row", "col"), None, None, None, None),
        P(("row", "col"), None, None),
    )
    out_specs = (P(("row", "col"), None), P(("row", "col"), None, None))
    return jax.shard_map(per_device, mesh=mesh, in_specs=in_specs, out_specs=out_specs, check_vma=False)
```

```python
import functools

import jax
import jax.numpy as jnp
from jax import lax
from jax.experimental import pallas as pl
from jax.experimental.pallas import tpu as pltpu
from jax.sharding import PartitionSpec as P

MESH = pl.DeviceIdType.MESH
F32 = jnp.float32
BF16 = jnp.bfloat16
I32 = jnp.int32
NN = (((1,), (0,)), ((), ()))
NT = (((1,), (1,)), ((), ()))

DEV = 128
LEVELS = 7
W = 256
R = 64
LEAF = 12
NCOUP = 4
ROWS = 3072
SEG = 24
HALF = 12
MSG = HALF + 1
SPREAD = 37
PARTS = 4
PART = R // PARTS
PITCH = 16


def mesh_id(device):
    return (lax.shift_right_logical(device, 4), device & 15)


def split(value):
    high = value.astype(BF16)
    return high, (value - high.astype(F32)).astype(BF16)


def pieces(x):
    high, low = split(x)
    return jnp.concatenate([high, low], 0), high


def dot3(x2, xh, weights, dims):
    wh, wl = split(weights)
    n = xh.shape[0]
    both = lax.dot_general(x2, wh, dims, preferred_element_type=F32)
    cross = lax.dot_general(xh, wl, dims, preferred_element_type=F32)
    return both[:n] + both[n:] + cross


def iota(shape, axis):
    return lax.broadcasted_iota(I32, shape, axis)


def within(index, size):
    return jnp.clip(index, 0, size - 1)


def onehot(mask):
    return jnp.where(mask, 1.0, 0.0)


def trailing_zeros(number):
    total = jnp.int32(0)
    for k in range(1, 8):
        total = total + jnp.where((number & ((1 << k) - 1)) == 0, 1, 0)
    return total


def gather_pairs(steps, source, table, first, second, store, lanes=range(128)):
    left = iota((1, 128), 1) < R

    def step(k, carry):
        for l in lanes:
            a = table[first(k), l]
            b = table[second(k), l]
            store(k, l, jnp.where(left, source[pl.ds(a, 1), :], source[pl.ds(b, 1), :]))
        return carry

    lax.fori_loop(0, steps, step, 0)


def swap_halves(both, first=0, count=DEV * PITCH):
    def group(g, carry):
        at = pl.multiple_of(first + g * 128, 128)
        both[pl.ds(at + DEV * PITCH, 128), :] = pltpu.roll(both[pl.ds(at, 128), :], R, 1)
        return carry

    lax.fori_loop(0, count // 128, group, 0, unroll=2)


def kernel(
    rhs_hbm, map_hbm, seprhs_hbm, sepinv_hbm, seppar_hbm, leafinv_hbm, coup_hbm, links,
    came_hbm, pos_hbm, sep_hbm,
    rhs, rmap, seprhs, sepinv, seppar, leafinv, coup,
    doubled, sbuf, received, grouped, solved, sbuf2,
    anc, crit, sepout, ready, acc, qt, cums, labels, pos_v, idx_v, idx, idx_r,
    in_sem, loc_sem, crit_send, crit_recv, part_recv, zero_send, zero_recv, four_send, four_recv, five_send, five_recv,
    scat_send, scat_recv, ag_send, ag_recv, a_send, a_recv, b_send, b_recv, gate,
):
    me = lax.axis_index("row") * 16 + lax.axis_index("col")

    loads = [
        pltpu.make_async_copy(s, d, in_sem.at[i])
        for i, (s, d) in enumerate(
            (
                (sepinv_hbm, sepinv), (seprhs_hbm, seprhs), (map_hbm, rmap), (seppar_hbm, seppar),
                (rhs_hbm, rhs), (coup_hbm, coup), (leafinv_hbm, leafinv),
            )
        )
    ]
    for load in loads:
        load.start()

    barrier = pltpu.get_barrier_semaphore()

    for k in [16 * i for i in range(1, 8)] + list(range(1, 16)):
        pl.semaphore_signal(barrier, inc=1, device_id=mesh_id(me ^ k), device_id_type=MESH)

    own = 6 - trailing_zeros(me + 1)
    reach = lax.shift_right_logical(jnp.int32(32), jnp.clip(own, 0, 5))
    inner = (own >= 0) & (own < 6)
    x_at = me & 3
    even = (me & 1) == 0

    def remote(src, dst, send, recv, to):
        return pltpu.make_async_remote_copy(
            src_ref=src, dst_ref=dst, send_sem=send, recv_sem=recv, device_id=mesh_id(to), device_id_type=MESH
        )

    def rows_of(first, count):
        return anc.at[pl.ds(pl.multiple_of(first, 8), count)]

    def drain(count, sem):
        pltpu.make_async_copy(anc.at[pl.ds(0, count)], anc.at[pl.ds(0, count)], sem).wait()

    def set_level(m, value):
        anc[m * R:(m + 1) * R, :] = value

    def send_part(h):
        part = pl.ds(h * PART, PART)

        @pl.when(inner)
        def _():
            remote(sepout.at[part], crit.at[part], crit_send.at[0], crit_recv.at[h], me - reach).start()
            remote(sepout.at[part], crit.at[part], crit_send.at[1], crit_recv.at[h], me + reach).start()

        @pl.when(own == 6)
        def _():
            remote(sepout.at[part], rows_of(6 * R + h * PART, PART), crit_send.at[0], part_recv, me + 1).start()

    def finish_children():
        drain(R, crit_send.at[0])
        drain(R, crit_send.at[1])

    def zero_to(to, which):
        return remote(crit, rows_of(0, R), zero_send.at[which], zero_recv, to)

    def four_to():
        return [
            remote(sepout, rows_of(4 * R, R), four_send.at[i], four_recv, (me & 120) | low)
            for i, low in enumerate((0, 2, 7, 4, 6))
        ]

    def five_to():
        return remote(sepout, rows_of(5 * R, R), five_send, five_recv, me + 2)

    def solve_part(h, target):
        t2, th = pieces(target)
        sepout[h * PART:(h + 1) * PART, :] = dot3(t2, th, sepinv[...], NT)

    def take_and_solve():
        for h in range(PARTS):
            rows = slice(h * PART, (h + 1) * PART)
            with jax.named_scope("parent_wait"):
                pltpu.make_async_copy(sepout.at[pl.ds(0, PART)], crit.at[pl.ds(0, PART)], crit_recv.at[h]).wait()
            with jax.named_scope("own_solve"):
                p2, ph = pieces(crit[rows, :])
                solve_part(h, seprhs[rows, :] - dot3(p2, ph, seppar[...], NN))
            send_part(h)

        @pl.when(own == 5)
        def _():
            five_to().start()

    def heard_first():
        pl.semaphore_wait(barrier, 22)

        for i in range(1, 8):
            pl.semaphore_signal(gate, inc=1, device_id=mesh_id(me ^ (16 * i)), device_id_type=MESH)

    loads[0].wait()
    loads[1].wait()

    @pl.when(own == 0)
    def _():
        for h in range(PARTS):
            solve_part(h, seprhs[h * PART:(h + 1) * PART, :])
        heard_first()
        for h in range(PARTS):
            send_part(h)

    @pl.when(own < 0)
    def _():
        sepout[...] = jnp.zeros_like(sepout)

    loads[2].wait()
    rows = rmap[...]
    dest = lax.shift_right_logical(lax.shift_right_logical(rows, 10) * 171, 9)
    local = rows - dest * ROWS
    for j in range(12):
        for h in range(2):
            r = 2 * j + h
            qt[j * 128:(j + 1) * 128, h * 128:(h + 1) * 128] = onehot(
                iota((128, 128), 0) == dest[r:r + 1, :]
            ).astype(BF16)
    tri = onehot((iota((256, 384), 0) < iota((256, 384), 1)) | (iota((256, 384), 1) >= 256)).astype(BF16)
    cums[...] = lax.dot_general(qt[...], tri, NN, preferred_element_type=F32)
    carry = jnp.zeros((128, 128), F32)
    table = jnp.zeros((128, 128), F32)
    sub32 = iota((32, 128), 0)
    lane = iota((1, 128), 1)
    for j in range(12):
        parts = []
        for h in range(2):
            r = 2 * j + h
            q = qt[j * 128:(j + 1) * 128, h * 128:(h + 1) * 128].astype(F32)
            rank = jnp.sum(q * (cums[j * 128:(j + 1) * 128, h * 128:(h + 1) * 128] + carry), axis=0, keepdims=True)
            rank = rank.astype(I32)
            hit = sub32 == rank
            loc = local[r:r + 1, :]
            parts.append(
                jnp.concatenate(
                    [
                        jnp.where(hit, float(r), 0.0),
                        jnp.where(hit, lane.astype(F32), 0.0),
                        jnp.where(hit, lax.shift_right_logical(loc, 7).astype(F32), 0.0),
                        jnp.where(hit, (loc & 127).astype(F32), 0.0),
                    ],
                    0,
                )
            )
            at = dest[r:r + 1, :] * PITCH + rank + jnp.where(rank >= HALF, DEV * PITCH - HALF, 0)
            pos_v[r:r + 1, :] = within(at, 2 * DEV * PITCH) ^ (h * DEV * PITCH)
        digits = jnp.concatenate(parts, 1).astype(BF16)
        table = table + lax.dot_general(digits, qt[j * 128:(j + 1) * 128, :], NT, preferred_element_type=F32)
        carry = carry + cums[j * 128:(j + 1) * 128, 256:384]
    idx_v[0:24, :] = within((table[0:24] * 128.0 + table[32:56]).astype(I32), ROWS)
    to_idx = pltpu.make_async_copy(idx_v.at[pl.ds(0, 24)], idx, loc_sem.at[0])
    to_idx.start()
    to_pos = pltpu.make_async_copy(pos_v, pos_hbm, loc_sem.at[1])
    to_pos.start()
    lab = table[64:96] * 128.0 + table[96:128]
    labels[...] = jnp.concatenate([lab, jnp.zeros((96, 128), F32)], 0).T

    loads[4].wait()

    def double_rhs(j, carry):
        block = rhs[:, pl.ds(pl.multiple_of(j * 128, 128), 128)]
        doubled[pl.ds(pl.multiple_of(j * 128, 128), 128), :] = jnp.concatenate([block, block], 0).T
        return carry

    lax.fori_loop(0, ROWS // 128, double_rhs, 0, unroll=4)

    to_idx.wait()

    def put_send(k, l, row):
        sbuf[pl.ds(l * PITCH + k, 1), :] = row

    def landing(dst, device, n):
        return dst.at[pl.ds(pl.multiple_of(device * PITCH, PITCH), n)]

    def exchange(core, src, dst, n, send, recv):
        def go(k, carry):
            j = (k * SPREAD) & 63
            to = (me ^ ((j & 15) + (j // 16) * 32)) & 111 | (core * 16)

            @pl.when(to != me)
            def _():
                remote(landing(src, to, n), landing(dst, me, n), send, recv, to).start()

            return carry

        lax.fori_loop(0, 64, go, 0)

    def lanes_of(core):
        return [l for l in range(DEV) if (l >> 4) & 1 == core]

    def exchange_wait(rows, n, sem):
        count = (DEV - 1) * n
        pltpu.make_async_copy(rows.at[pl.ds(0, count)], rows.at[pl.ds(0, count)], sem).wait()

    @pl.when(own != 0)
    def _():
        heard_first()

    loads[3].wait()

    @pl.when(own == 1)
    def _():
        take_and_solve()
        zero_to(me - reach, 0).start()
        zero_to(me + reach, 1).start()

    gather_pairs(HALF, doubled, idx, lambda k: k, lambda k: k + HALF, put_send)
    for l in range(DEV):
        sbuf[l * PITCH + HALF:l * PITCH + MSG, :] = labels[l:l + 1, :]
    pl.semaphore_wait(gate, 7)

    @pl.when(own == 0)
    def _():
        finish_children()

    @pl.when(own == 2)
    def _():
        take_and_solve()

    @pl.when(own == 2)
    def _():
        set_level(1, crit[...])
        set_level(2, sepout[...])
        drain(R, zero_recv)

        def tile(i, carry):
            to = (me & 96) | (i // 3 * 4 + i % 3)
            remote(rows_of(i * 8, 8), rows_of(i * 8, 8), scat_send, scat_recv.at[0], to).start()
            return carry

        lax.fori_loop(0, 24, tile, 0)

    for core in range(2):
        exchange(core, sbuf, received, MSG, a_send, a_recv)
    keep = pltpu.make_async_copy(landing(sbuf, me, MSG), landing(received, me, MSG), loc_sem.at[2])
    keep.start()

    @pl.when(own == 3)
    def _():
        take_and_solve()
        set_level(3, sepout[...])
        for i in range(8):
            part = rows_of(3 * R + 8 * i, 8)
            remote(part, part, scat_send, scat_recv.at[1], (me & 112) | (i // 2 * 4 + i % 2 * 2)).start()

    @pl.when(own == 4)
    def _():
        take_and_solve()
        set_level(4, sepout[...])
        finish_children()
        for c in four_to():
            c.start()

    @pl.when(x_at != 3)
    def _():
        drain(8, scat_recv.at[0])
        part = rows_of((lax.shift_right_logical(me, 2) & 7) * 24 + x_at * 8, 8)

        def hand(k, carry):
            to = me ^ k

            @pl.when((to & 31) != 15)
            def _():
                remote(part, part, ag_send.at[0], ag_recv.at[0], to).start()

            return carry

        lax.fori_loop(1, 32, hand, 0)

    @pl.when(even)
    def _():
        drain(8, scat_recv.at[1])
        part = rows_of(3 * R + (lax.shift_right_logical(me, 2) & 3) * 16 + x_at * 4, 8)

        def hand(k, carry):
            to = me ^ k

            @pl.when((to & 15) != 7)
            def _():
                remote(part, part, ag_send.at[1], ag_recv.at[1], to).start()

            return carry

        lax.fori_loop(1, 16, hand, 0)

    exchange_wait(doubled, MSG, a_recv)
    keep.wait()
    for p in range(128):
        labels[p:p + 1, :] = received[p * PITCH + HALF:p * PITCH + MSG, :]
    got = labels[...].T[0:32].astype(I32)
    high = lax.shift_right_logical(got, 7)
    low = got & 127
    inverse = jnp.zeros((64, 128), F32)
    for j in range(12):
        aa, bb = [], []
        for h in range(2):
            r = 2 * j + h
            at = lane * PITCH + (r % HALF + (r // HALF) * DEV * PITCH)
            hit = sub32 == high[r:r + 1, :]
            aa.append(
                jnp.concatenate(
                    [
                        jnp.where(hit, lax.shift_right_logical(at, 6).astype(F32), 0.0),
                        jnp.where(hit, (at & 63).astype(F32), 0.0),
                    ],
                    0,
                )
            )
            bb.append(onehot(iota((128, 128), 0) == low[r:r + 1, :]))
        inverse = inverse + lax.dot_general(
            jnp.concatenate(aa, 1).astype(BF16), jnp.concatenate(bb, 1).astype(BF16), NT, preferred_element_type=F32
        )
    found_at = within((inverse[0:24] * 64.0 + inverse[32:56]).astype(I32), 2 * DEV * PITCH)
    idx_v[0:24, :] = found_at ^ ((iota((24, 128), 0) & 1) * (DEV * PITCH))
    idx_v[24:48, :] = within(((high & 1) * (ROWS // 2) + lax.shift_right_logical(high, 1) * 128 + low)[0:24], ROWS)
    to_idx = pltpu.make_async_copy(idx_v, idx_r, loc_sem.at[0])
    to_idx.start()

    swap_halves(received)
    @pl.when(own == 5)
    def _():
        take_and_solve()
        set_level(4, crit[...])
        set_level(5, sepout[...])

    to_idx.wait()

    def put_grouped(k, l, row):
        grouped[pl.ds(k * 128 + l, 1), :] = row

    gather_pairs(LEAF, received, idx_r, lambda k: 2 * k, lambda k: 2 * k + 1, put_grouped)

    @pl.when(own == 6)
    def _():
        take_and_solve()
        set_level(5, crit[...])
        set_level(6, sepout[...])

    loads[5].wait()

    def make_ready(m):
        x2, _ = pieces(anc[m * R:(m + 1) * R, :])
        ready[m] = x2

    def block(i):
        def blocks(g, carry):
            for u in range(4):
                s = g * 4 + u
                link = [links[c, s] for c in range(NCOUP)]
                which = jnp.int32(0)
                level = jnp.int32(0)
                for c in range(NCOUP):
                    above = jnp.int32(0)
                    for other in range(NCOUP):
                        if other != c:
                            above = above + jnp.where(link[other] > link[c], 1, 0)
                    which = jnp.where(above == i, c, which)
                    level = jnp.where(above == i, LEVELS - 1 - link[c], level)
                x2 = ready[level]
                term = dot3(x2, x2[:R], coup[s * NCOUP + which], NN)
                acc[s] = term if i == 0 else acc[s] + term
            return carry

        lax.fori_loop(0, LEAF // 4, blocks, 0)

    @pl.when((x_at != 3))
    def _():
        drain(184, ag_recv.at[0])

    @pl.when((x_at == 3) & (own != 2))
    def _():
        drain(192, ag_recv.at[0])

    @pl.when(even)
    def _():
        drain(56, ag_recv.at[1])

    @pl.when(~even & ((me & 15) != 7))
    def _():
        drain(64, ag_recv.at[1])

    for m in range(4):
        make_ready(m)
    block(0)

    @pl.when(even | ((me & 7) == 7))
    def _():
        drain(R, four_recv)

    make_ready(4)
    block(1)

    @pl.when(x_at == 3)
    def _():
        drain(R, five_recv)

    make_ready(5)
    block(2)

    @pl.when(~even)
    def _():
        drain(R, part_recv)

    make_ready(6)
    block(3)

    loads[6].wait()

    def leaf(g, carry):
        for u in range(4):
            t = g * 4 + u
            at = pl.multiple_of(t * 128, 128)
            both = grouped[pl.ds(at, 128), :].T
            target = jnp.concatenate([both[:R], both[R:]], 1) - acc[t]
            t2, th = pieces(target)
            x = dot3(t2, th, leafinv[t], NT)
            solved[pl.ds(at, 128), :] = jnp.concatenate([x[:, :128], x[:, :128]], 0).T
            solved[pl.ds(pl.multiple_of(at + ROWS // 2, 128), 128), :] = jnp.concatenate([x[:, 128:], x[:, 128:]], 0).T
        return carry

    lax.fori_loop(0, LEAF // 4, leaf, 0)

    def put_back(k, l, row):
        sbuf2[pl.ds(l * PITCH + k, 1), :] = row

    for core in range(2):
        gather_pairs(HALF, solved, idx_r, lambda k: k + 24, lambda k: k + 24 + HALF, put_back, lanes_of(core))
        exchange(core, sbuf2, came_hbm, HALF, b_send, b_recv)
    mine = pltpu.make_async_copy(landing(sbuf2, me, HALF), landing(came_hbm, me, HALF), loc_sem.at[2])
    mine.start()
    out_sep = pltpu.make_async_copy(sepout, sep_hbm, loc_sem.at[3])
    out_sep.start()

    exchange_wait(doubled, MSG, a_send)

    @pl.when(own == 6)
    def _():
        drain(R, crit_send.at[0])

    @pl.when(own == 5)
    def _():
        five_to().wait_send()

    @pl.when(((own >= 1) & (own <= 3)) | (own == 5))
    def _():
        finish_children()

    @pl.when(own == 1)
    def _():
        zero_to(me - reach, 0).wait_send()
        zero_to(me + reach, 1).wait_send()

    @pl.when(own == 2)
    def _():
        drain(192, scat_send)

    @pl.when(own == 3)
    def _():
        drain(64, scat_send)

    @pl.when(own == 4)
    def _():
        for c in four_to():
            c.wait_send()

    @pl.when(x_at != 3)
    def _():
        drain(240, ag_send.at[0])

    @pl.when(even)
    def _():
        drain(112, ag_send.at[1])

    to_pos.wait()
    out_sep.wait()
    mine.wait()
    exchange_wait(doubled, HALF, b_recv)
    exchange_wait(doubled, HALF, b_send)


def restore_kernel(came_hbm, pos, sep_hbm, x_hbm, sepx_hbm, came, grouped, xout, sem, out_sem):
    part = DEV * PITCH // 4
    loads = [
        pltpu.make_async_copy(came_hbm.at[pl.ds(i * part, part)], came.at[pl.ds(i * part, part)], sem.at[2 + i])
        for i in range(4)
    ]
    for load in loads:
        load.start()
    move = pltpu.make_async_copy(sep_hbm, sepx_hbm, sem.at[1])
    move.start()
    with jax.named_scope("load_and_swap"):
        for i in range(4):
            loads[i].wait()
            swap_halves(came, i * part, part)
    left = iota((1, 128), 1) < R

    def pick(j, slot):
        for l in range(128):
            a = pos[2 * j, l]
            b = pos[2 * j + 1, l]
            grouped[slot, l:l + 1, :] = jnp.where(left, came[pl.ds(a, 1), :], came[pl.ds(b, 1), :])

    def write(j, slot):
        at = pl.ds(pl.multiple_of(j * 256, 256), 256)
        both = grouped[slot].T
        xout[:, at] = jnp.concatenate([both[:R], both[R:]], 1)
        pltpu.make_async_copy(xout.at[:, at], x_hbm.at[:, at], out_sem).start()

    with jax.named_scope("pick_first"):
        pick(0, 0)

    def step(i, carry):
        j = 2 * i
        pick(j + 1, 1)
        write(j, 0)
        pick(jnp.minimum(j + 2, LEAF - 1), 0)
        write(j + 1, 1)
        return carry

    with jax.named_scope("pick_and_write"):
        lax.fori_loop(0, LEAF // 2, step, 0)
    with jax.named_scope("drain"):
        pltpu.make_async_copy(xout, x_hbm, out_sem).wait()
        move.wait()


def per_device(rhs_held, row_map, sep_rhs, sep_inverse, sep_parent, leaf_inverse, leaf_coupling, leaf_links):
    hbm = pl.BlockSpec(memory_space=pltpu.HBM)
    vmem = pltpu.VMEM
    came, pos, sep = pl.pallas_call(
        kernel,
        out_shape=(
            jax.ShapeDtypeStruct((DEV * PITCH, 128), F32),
            jax.ShapeDtypeStruct((24, 128), I32),
            jax.ShapeDtypeStruct((R, W), F32),
        ),
        in_specs=[hbm] * 7 + [pl.BlockSpec(memory_space=pltpu.SMEM)],
        out_specs=(hbm, hbm, hbm),
        scratch_shapes=[
            vmem((R, ROWS), F32),
            vmem((24, 128), I32),
            vmem((R, W), F32),
            vmem((W, W), F32),
            vmem((W, W), F32),
            vmem((LEAF, W, W), F32),
            vmem((LEAF * NCOUP, W, W), F32),
            vmem((ROWS, 128), F32),
            vmem((DEV * PITCH, 128), F32),
            vmem((2 * DEV * PITCH, 128), F32),
            vmem((ROWS // 2, 128), F32),
            vmem((ROWS, 128), F32),
            vmem((DEV * PITCH, 128), F32),
            vmem((LEVELS * R, W), F32),
            vmem((R, W), F32),
            vmem((R, W), F32),
            vmem((LEVELS, 2 * R, W), BF16),
            vmem((LEAF, R, W), F32),
            vmem((12 * 128, 256), BF16),
            vmem((12 * 128, 384), F32),
            vmem((128, 128), F32),
            vmem((24, 128), I32),
            vmem((48, 128), I32),
            pltpu.SMEM((24, 128), I32),
            pltpu.SMEM((48, 128), I32),
            pltpu.SemaphoreType.DMA((7,)),
            pltpu.SemaphoreType.DMA((4,)),
            pltpu.SemaphoreType.DMA((2,)),
            pltpu.SemaphoreType.DMA((PARTS,)),
            pltpu.SemaphoreType.DMA,
            pltpu.SemaphoreType.DMA((2,)),
            pltpu.SemaphoreType.DMA,
            pltpu.SemaphoreType.DMA((5,)),
            pltpu.SemaphoreType.DMA,
            pltpu.SemaphoreType.DMA,
            pltpu.SemaphoreType.DMA,
            pltpu.SemaphoreType.DMA,
            pltpu.SemaphoreType.DMA((2,)),
            pltpu.SemaphoreType.DMA((2,)),
            pltpu.SemaphoreType.DMA((2,)),
            pltpu.SemaphoreType.DMA,
            pltpu.SemaphoreType.DMA,
            pltpu.SemaphoreType.DMA,
            pltpu.SemaphoreType.DMA,
            pltpu.SemaphoreType.REGULAR,
        ],
        compiler_params=pltpu.CompilerParams(
            collective_id=0, has_side_effects=True, vmem_limit_bytes=56 << 20
        ),
        name="gmrf_solve",
    )(
        rhs_held.T,
        row_map.reshape(24, 128),
        sep_rhs[0].T,
        sep_inverse[0],
        sep_parent[0],
        leaf_inverse[0],
        leaf_coupling[0].reshape(LEAF * NCOUP, W, W),
        leaf_links[0].T,
    )
    x, sep = pl.pallas_call(
        restore_kernel,
        out_shape=(jax.ShapeDtypeStruct((R, ROWS), F32), jax.ShapeDtypeStruct((R, W), F32)),
        in_specs=[hbm, pl.BlockSpec(memory_space=pltpu.SMEM), hbm],
        out_specs=(hbm, hbm),
        scratch_shapes=[
            vmem((2 * DEV * PITCH, 128), F32),
            vmem((2, 128, 128), F32),
            vmem((R, ROWS), F32),
            pltpu.SemaphoreType.DMA((6,)),
            pltpu.SemaphoreType.DMA,
        ],
        compiler_params=pltpu.CompilerParams(vmem_limit_bytes=56 << 20),
        name="restore_rows",
    )(came, pos, sep)
    return x.T, sep.T[None]


def solution(mesh):
    in_specs = (
        P(("row", "col"), None),
        P(("row", "col")),
        P(("row", "col"), None, None),
        P(("row", "col"), None, None),
        P(("row", "col"), None, None),
        P(("row", "col"), None, None, None),
        P(("row", "col"), None, None, None, None),
        P(("row", "col"), None, None),
    )
    out_specs = (P(("row", "col"), None), P(("row", "col"), None, None))
    return jax.shard_map(per_device, mesh=mesh, in_specs=in_specs, out_specs=out_specs, check_vma=False)
```

```python
import functools

import jax
import jax.numpy as jnp
from jax import lax
from jax.experimental import pallas as pl
from jax.experimental.pallas import tpu as pltpu
from jax.sharding import PartitionSpec as P

MESH = pl.DeviceIdType.MESH
F32 = jnp.float32
BF16 = jnp.bfloat16
I32 = jnp.int32
NN = (((1,), (0,)), ((), ()))
NT = (((1,), (1,)), ((), ()))

DEV = 128
LEVELS = 7
W = 256
R = 64
LEAF = 12
NCOUP = 4
ROWS = 3072
SEG = 24
HALF = 12
MSG = HALF + 1
BLOCK_STEP = 12
LEAF_STEP = 12
SPREAD = 37
PARTS = 4
PART = R // PARTS
PITCH = 16


def mesh_id(device):
    return (lax.shift_right_logical(device, 4), device & 15)


def split(value):
    high = value.astype(BF16)
    return high, (value - high.astype(F32)).astype(BF16)


def pieces(x):
    high, low = split(x)
    return jnp.concatenate([high, low], 0), high


def dot3(x2, xh, weights, dims):
    wh, wl = split(weights)
    n = xh.shape[0]
    both = lax.dot_general(x2, wh, dims, preferred_element_type=F32)
    cross = lax.dot_general(xh, wl, dims, preferred_element_type=F32)
    return both[:n] + both[n:] + cross


def iota(shape, axis):
    return lax.broadcasted_iota(I32, shape, axis)


def within(index, size):
    return jnp.clip(index, 0, size - 1)


def onehot(mask):
    return jnp.where(mask, 1.0, 0.0)


def trailing_zeros(number):
    total = jnp.int32(0)
    for k in range(1, 8):
        total = total + jnp.where((number & ((1 << k) - 1)) == 0, 1, 0)
    return total


def gather_pairs(steps, source, table, first, second, store, lanes=range(128)):
    left = iota((1, 128), 1) < R

    def step(k, carry):
        for l in lanes:
            a = table[first(k), l]
            b = table[second(k), l]
            store(k, l, jnp.where(left, source[pl.ds(a, 1), :], source[pl.ds(b, 1), :]))
        return carry

    lax.fori_loop(0, steps, step, 0)


def swap_halves(both, first=0, count=DEV * PITCH):
    def group(g, carry):
        at = pl.multiple_of(first + g * 128, 128)
        both[pl.ds(at + DEV * PITCH, 128), :] = pltpu.roll(both[pl.ds(at, 128), :], R, 1)
        return carry

    lax.fori_loop(0, count // 128, group, 0, unroll=4)


def kernel(
    rhs_hbm, map_hbm, seprhs_hbm, sepinv_hbm, seppar_hbm, leafinv_hbm, coup_hbm, links,
    came_hbm, pos_hbm, sep_hbm,
    rhs, rmap, seprhs, sepinv, seppar, leafinv, coup,
    doubled, sbuf, received, grouped, solved, sbuf2,
    anc, crit, sepout, ready, acc, qt, cums, labels, pos_v, idx_v, idx, idx_r,
    in_sem, loc_sem, crit_send, crit_recv, part_recv, zero_send, zero_recv, four_send, four_recv, five_send, five_recv,
    scat_send, scat_recv, ag_send, ag_recv, a_send, a_recv, b_send, b_recv, gate,
):
    me = lax.axis_index("row") * 16 + lax.axis_index("col")

    loads = [
        pltpu.make_async_copy(s, d, in_sem.at[i])
        for i, (s, d) in enumerate(
            (
                (sepinv_hbm, sepinv), (seprhs_hbm, seprhs), (map_hbm, rmap), (seppar_hbm, seppar),
                (rhs_hbm, rhs), (coup_hbm, coup), (leafinv_hbm, leafinv),
            )
        )
    ]
    for load in loads:
        load.start()

    barrier = pltpu.get_barrier_semaphore()

    for k in [16 * i for i in range(1, 8)] + list(range(1, 16)):
        pl.semaphore_signal(barrier, inc=1, device_id=mesh_id(me ^ k), device_id_type=MESH)

    own = 6 - trailing_zeros(me + 1)
    reach = lax.shift_right_logical(jnp.int32(32), jnp.clip(own, 0, 5))
    inner = (own >= 0) & (own < 6)
    x_at = me & 3
    even = (me & 1) == 0

    def remote(src, dst, send, recv, to):
        return pltpu.make_async_remote_copy(
            src_ref=src, dst_ref=dst, send_sem=send, recv_sem=recv, device_id=mesh_id(to), device_id_type=MESH
        )

    def rows_of(first, count):
        return anc.at[pl.ds(pl.multiple_of(first, 8), count)]

    def drain(count, sem):
        pltpu.make_async_copy(anc.at[pl.ds(0, count)], anc.at[pl.ds(0, count)], sem).wait()

    def set_level(m, value):
        anc[m * R:(m + 1) * R, :] = value

    def send_part(h):
        part = pl.ds(h * PART, PART)

        @pl.when(inner)
        def _():
            remote(sepout.at[part], crit.at[part], crit_send.at[0], crit_recv.at[h], me - reach).start()
            remote(sepout.at[part], crit.at[part], crit_send.at[1], crit_recv.at[h], me + reach).start()

        @pl.when(own == 6)
        def _():
            remote(sepout.at[part], rows_of(6 * R + h * PART, PART), crit_send.at[0], part_recv, me + 1).start()

    def finish_children():
        drain(R, crit_send.at[0])
        drain(R, crit_send.at[1])

    def zero_to(to, which):
        return remote(crit, rows_of(0, R), zero_send.at[which], zero_recv, to)

    def four_to():
        return [
            remote(sepout, rows_of(4 * R, R), four_send.at[i], four_recv, (me & 120) | low)
            for i, low in enumerate((0, 2, 7, 4, 6))
        ]

    def five_to():
        return remote(sepout, rows_of(5 * R, R), five_send, five_recv, me + 2)

    def solve_part(h, target):
        t2, th = pieces(target)
        sepout[h * PART:(h + 1) * PART, :] = dot3(t2, th, sepinv[...], NT)

    def take_and_solve():
        for h in range(PARTS):
            rows = slice(h * PART, (h + 1) * PART)
            with jax.named_scope("parent_wait"):
                pltpu.make_async_copy(sepout.at[pl.ds(0, PART)], crit.at[pl.ds(0, PART)], crit_recv.at[h]).wait()
            with jax.named_scope("own_solve"):
                p2, ph = pieces(crit[rows, :])
                solve_part(h, seprhs[rows, :] - dot3(p2, ph, seppar[...], NN))
            send_part(h)

        @pl.when(own == 5)
        def _():
            five_to().start()

    def heard_first():
        pl.semaphore_wait(barrier, 22)

        for i in range(1, 8):
            pl.semaphore_signal(gate, inc=1, device_id=mesh_id(me ^ (16 * i)), device_id_type=MESH)

    loads[0].wait()
    loads[1].wait()

    @pl.when(own == 0)
    def _():
        for h in range(PARTS):
            solve_part(h, seprhs[h * PART:(h + 1) * PART, :])
        heard_first()
        for h in range(PARTS):
            send_part(h)

    @pl.when(own < 0)
    def _():
        sepout[...] = jnp.zeros_like(sepout)

    loads[2].wait()
    rows = rmap[...]
    dest = lax.shift_right_logical(lax.shift_right_logical(rows, 10) * 171, 9)
    local = rows - dest * ROWS
    for j in range(12):
        for h in range(2):
            r = 2 * j + h
            qt[j * 128:(j + 1) * 128, h * 128:(h + 1) * 128] = onehot(
                iota((128, 128), 0) == dest[r:r + 1, :]
            ).astype(BF16)
    tri = onehot((iota((256, 384), 0) < iota((256, 384), 1)) | (iota((256, 384), 1) >= 256)).astype(BF16)
    cums[...] = lax.dot_general(qt[...], tri, NN, preferred_element_type=F32)
    carry = jnp.zeros((128, 128), F32)
    table = jnp.zeros((128, 128), F32)
    sub32 = iota((32, 128), 0)
    lane = iota((1, 128), 1)
    for j in range(12):
        parts = []
        for h in range(2):
            r = 2 * j + h
            q = qt[j * 128:(j + 1) * 128, h * 128:(h + 1) * 128].astype(F32)
            rank = jnp.sum(q * (cums[j * 128:(j + 1) * 128, h * 128:(h + 1) * 128] + carry), axis=0, keepdims=True)
            rank = rank.astype(I32)
            hit = sub32 == rank
            loc = local[r:r + 1, :]
            parts.append(
                jnp.concatenate(
                    [
                        jnp.where(hit, float(r), 0.0),
                        jnp.where(hit, lane.astype(F32), 0.0),
                        jnp.where(hit, lax.shift_right_logical(loc, 7).astype(F32), 0.0),
                        jnp.where(hit, (loc & 127).astype(F32), 0.0),
                    ],
                    0,
                )
            )
            at = dest[r:r + 1, :] * PITCH + rank + jnp.where(rank >= HALF, DEV * PITCH - HALF, 0)
            pos_v[r:r + 1, :] = within(at, 2 * DEV * PITCH) ^ (h * DEV * PITCH)
        digits = jnp.concatenate(parts, 1).astype(BF16)
        table = table + lax.dot_general(digits, qt[j * 128:(j + 1) * 128, :], NT, preferred_element_type=F32)
        carry = carry + cums[j * 128:(j + 1) * 128, 256:384]
    idx_v[0:24, :] = within((table[0:24] * 128.0 + table[32:56]).astype(I32), ROWS)
    to_idx = pltpu.make_async_copy(idx_v.at[pl.ds(0, 24)], idx, loc_sem.at[0])
    to_idx.start()
    to_pos = pltpu.make_async_copy(pos_v, pos_hbm, loc_sem.at[1])
    to_pos.start()
    lab = table[64:96] * 128.0 + table[96:128]
    labels[...] = jnp.concatenate([lab, jnp.zeros((96, 128), F32)], 0).T

    loads[4].wait()

    def double_rhs(j, carry):
        block = rhs[:, pl.ds(pl.multiple_of(j * 128, 128), 128)]
        doubled[pl.ds(pl.multiple_of(j * 128, 128), 128), :] = jnp.concatenate([block, block], 0).T
        return carry

    lax.fori_loop(0, ROWS // 128, double_rhs, 0, unroll=12)

    to_idx.wait()

    def put_send(k, l, row):
        sbuf[pl.ds(l * PITCH + k, 1), :] = row

    def landing(dst, device, n):
        return dst.at[pl.ds(pl.multiple_of(device * PITCH, PITCH), n)]

    def exchange(core, src, dst, n, send, recv):
        def go(k, carry):
            j = (k * SPREAD) & 63
            to = (me ^ ((j & 15) + (j // 16) * 32)) & 111 | (core * 16)

            @pl.when(to != me)
            def _():
                remote(landing(src, to, n), landing(dst, me, n), send, recv, to).start()

            return carry

        lax.fori_loop(0, 64, go, 0)

    def lanes_of(core):
        return [l for l in range(DEV) if (l >> 4) & 1 == core]

    def exchange_wait(rows, n, sem):
        count = (DEV - 1) * n
        pltpu.make_async_copy(rows.at[pl.ds(0, count)], rows.at[pl.ds(0, count)], sem).wait()

    @pl.when(own != 0)
    def _():
        heard_first()

    loads[3].wait()

    @pl.when(own == 1)
    def _():
        take_and_solve()
        zero_to(me - reach, 0).start()
        zero_to(me + reach, 1).start()

    gather_pairs(HALF, doubled, idx, lambda k: k, lambda k: k + HALF, put_send)
    for l in range(DEV):
        sbuf[l * PITCH + HALF:l * PITCH + MSG, :] = labels[l:l + 1, :]
    pl.semaphore_wait(gate, 7)

    @pl.when(own == 0)
    def _():
        finish_children()

    @pl.when(own == 2)
    def _():
        take_and_solve()

    @pl.when(own == 2)
    def _():
        set_level(1, crit[...])
        set_level(2, sepout[...])
        drain(R, zero_recv)

        def tile(i, carry):
            to = (me & 96) | (i // 3 * 4 + i % 3)
            remote(rows_of(i * 8, 8), rows_of(i * 8, 8), scat_send, scat_recv.at[0], to).start()
            return carry

        lax.fori_loop(0, 24, tile, 0)

    for core in range(2):
        exchange(core, sbuf, received, MSG, a_send, a_recv)
    keep = pltpu.make_async_copy(landing(sbuf, me, MSG), landing(received, me, MSG), loc_sem.at[2])
    keep.start()

    @pl.when(own == 3)
    def _():
        take_and_solve()
        set_level(3, sepout[...])
        for i in range(8):
            part = rows_of(3 * R + 8 * i, 8)
            remote(part, part, scat_send, scat_recv.at[1], (me & 112) | (i // 2 * 4 + i % 2 * 2)).start()

    @pl.when(own == 4)
    def _():
        take_and_solve()
        set_level(4, sepout[...])
        finish_children()
        for c in four_to():
            c.start()

    @pl.when(x_at != 3)
    def _():
        drain(8, scat_recv.at[0])
        part = rows_of((lax.shift_right_logical(me, 2) & 7) * 24 + x_at * 8, 8)

        def hand(k, carry):
            to = me ^ k

            @pl.when((to & 31) != 15)
            def _():
                remote(part, part, ag_send.at[0], ag_recv.at[0], to).start()

            return carry

        lax.fori_loop(1, 32, hand, 0)

    @pl.when(even)
    def _():
        drain(8, scat_recv.at[1])
        part = rows_of(3 * R + (lax.shift_right_logical(me, 2) & 3) * 16 + x_at * 4, 8)

        def hand(k, carry):
            to = me ^ k

            @pl.when((to & 15) != 7)
            def _():
                remote(part, part, ag_send.at[1], ag_recv.at[1], to).start()

            return carry

        lax.fori_loop(1, 16, hand, 0)

    exchange_wait(doubled, MSG, a_recv)
    keep.wait()
    for p in range(128):
        labels[p:p + 1, :] = received[p * PITCH + HALF:p * PITCH + MSG, :]
    got = labels[...].T[0:32].astype(I32)
    high = lax.shift_right_logical(got, 7)
    low = got & 127
    inverse = jnp.zeros((64, 128), F32)
    for j in range(12):
        aa, bb = [], []
        for h in range(2):
            r = 2 * j + h
            at = lane * PITCH + (r % HALF + (r // HALF) * DEV * PITCH)
            hit = sub32 == high[r:r + 1, :]
            aa.append(
                jnp.concatenate(
                    [
                        jnp.where(hit, lax.shift_right_logical(at, 6).astype(F32), 0.0),
                        jnp.where(hit, (at & 63).astype(F32), 0.0),
                    ],
                    0,
                )
            )
            bb.append(onehot(iota((128, 128), 0) == low[r:r + 1, :]))
        inverse = inverse + lax.dot_general(
            jnp.concatenate(aa, 1).astype(BF16), jnp.concatenate(bb, 1).astype(BF16), NT, preferred_element_type=F32
        )
    found_at = within((inverse[0:24] * 64.0 + inverse[32:56]).astype(I32), 2 * DEV * PITCH)
    idx_v[0:24, :] = found_at ^ ((iota((24, 128), 0) & 1) * (DEV * PITCH))
    idx_v[24:48, :] = within(((high & 1) * (ROWS // 2) + lax.shift_right_logical(high, 1) * 128 + low)[0:24], ROWS)
    to_idx = pltpu.make_async_copy(idx_v, idx_r, loc_sem.at[0])
    to_idx.start()

    swap_halves(received)
    @pl.when(own == 5)
    def _():
        take_and_solve()
        set_level(4, crit[...])
        set_level(5, sepout[...])

    to_idx.wait()

    def put_grouped(k, l, row):
        grouped[pl.ds(k * 128 + l, 1), :] = row

    gather_pairs(LEAF, received, idx_r, lambda k: 2 * k, lambda k: 2 * k + 1, put_grouped)

    @pl.when(own == 6)
    def _():
        take_and_solve()
        set_level(5, crit[...])
        set_level(6, sepout[...])

    loads[5].wait()

    def make_ready(m):
        x2, _ = pieces(anc[m * R:(m + 1) * R, :])
        ready[m] = x2

    def block(i):
        def blocks(g, carry):
            for u in range(BLOCK_STEP):
                s = g * BLOCK_STEP + u
                link = [links[c, s] for c in range(NCOUP)]
                which = jnp.int32(0)
                level = jnp.int32(0)
                for c in range(NCOUP):
                    above = jnp.int32(0)
                    for other in range(NCOUP):
                        if other != c:
                            above = above + jnp.where(link[other] > link[c], 1, 0)
                    which = jnp.where(above == i, c, which)
                    level = jnp.where(above == i, LEVELS - 1 - link[c], level)
                x2 = ready[level]
                term = dot3(x2, x2[:R], coup[s * NCOUP + which], NN)
                acc[s] = term if i == 0 else acc[s] + term
            return carry

        lax.fori_loop(0, LEAF // BLOCK_STEP, blocks, 0)

    @pl.when((x_at != 3))
    def _():
        drain(184, ag_recv.at[0])

    @pl.when((x_at == 3) & (own != 2))
    def _():
        drain(192, ag_recv.at[0])

    @pl.when(even)
    def _():
        drain(56, ag_recv.at[1])

    @pl.when(~even & ((me & 15) != 7))
    def _():
        drain(64, ag_recv.at[1])

    for m in range(4):
        make_ready(m)
    block(0)

    @pl.when(even | ((me & 7) == 7))
    def _():
        drain(R, four_recv)

    make_ready(4)
    block(1)

    @pl.when(x_at == 3)
    def _():
        drain(R, five_recv)

    make_ready(5)
    block(2)

    @pl.when(~even)
    def _():
        drain(R, part_recv)

    make_ready(6)
    block(3)

    loads[6].wait()

    def leaf(g, carry):
        for u in range(LEAF_STEP):
            t = g * LEAF_STEP + u
            at = pl.multiple_of(t * 128, 128)
            both = grouped[pl.ds(at, 128), :].T
            target = jnp.concatenate([both[:R], both[R:]], 1) - acc[t]
            t2, th = pieces(target)
            x = dot3(t2, th, leafinv[t], NT)
            solved[pl.ds(at, 128), :] = jnp.concatenate([x[:, :128], x[:, :128]], 0).T
            solved[pl.ds(pl.multiple_of(at + ROWS // 2, 128), 128), :] = jnp.concatenate([x[:, 128:], x[:, 128:]], 0).T
        return carry

    lax.fori_loop(0, LEAF // LEAF_STEP, leaf, 0)

    def put_back(k, l, row):
        sbuf2[pl.ds(l * PITCH + k, 1), :] = row

    for core in range(2):
        gather_pairs(HALF, solved, idx_r, lambda k: k + 24, lambda k: k + 24 + HALF, put_back, lanes_of(core))
        exchange(core, sbuf2, came_hbm, HALF, b_send, b_recv)
    mine = pltpu.make_async_copy(landing(sbuf2, me, HALF), landing(came_hbm, me, HALF), loc_sem.at[2])
    mine.start()
    out_sep = pltpu.make_async_copy(sepout, sep_hbm, loc_sem.at[3])
    out_sep.start()

    exchange_wait(doubled, MSG, a_send)

    @pl.when(own == 6)
    def _():
        drain(R, crit_send.at[0])

    @pl.when(own == 5)
    def _():
        five_to().wait_send()

    @pl.when(((own >= 1) & (own <= 3)) | (own == 5))
    def _():
        finish_children()

    @pl.when(own == 1)
    def _():
        zero_to(me - reach, 0).wait_send()
        zero_to(me + reach, 1).wait_send()

    @pl.when(own == 2)
    def _():
        drain(192, scat_send)

    @pl.when(own == 3)
    def _():
        drain(64, scat_send)

    @pl.when(own == 4)
    def _():
        for c in four_to():
            c.wait_send()

    @pl.when(x_at != 3)
    def _():
        drain(240, ag_send.at[0])

    @pl.when(even)
    def _():
        drain(112, ag_send.at[1])

    to_pos.wait()
    out_sep.wait()
    mine.wait()
    exchange_wait(doubled, HALF, b_recv)
    exchange_wait(doubled, HALF, b_send)


def restore_kernel(came_hbm, pos, sep_hbm, x_hbm, sepx_hbm, came, grouped, xout, sem, out_sem):
    part = DEV * PITCH // 4
    loads = [
        pltpu.make_async_copy(came_hbm.at[pl.ds(i * part, part)], came.at[pl.ds(i * part, part)], sem.at[2 + i])
        for i in range(4)
    ]
    for load in loads:
        load.start()
    move = pltpu.make_async_copy(sep_hbm, sepx_hbm, sem.at[1])
    move.start()
    with jax.named_scope("load_and_swap"):
        for i in range(4):
            loads[i].wait()
            swap_halves(came, i * part, part)
    left = iota((1, 128), 1) < R

    def pick(j, slot):
        for l in range(128):
            a = pos[2 * j, l]
            b = pos[2 * j + 1, l]
            grouped[slot, l:l + 1, :] = jnp.where(left, came[pl.ds(a, 1), :], came[pl.ds(b, 1), :])

    def write(j, slot):
        at = pl.ds(pl.multiple_of(j * 256, 256), 256)
        both = grouped[slot].T
        xout[:, at] = jnp.concatenate([both[:R], both[R:]], 1)
        pltpu.make_async_copy(xout.at[:, at], x_hbm.at[:, at], out_sem).start()

    with jax.named_scope("pick_first"):
        pick(0, 0)

    def step(i, carry):
        j = 2 * i
        pick(j + 1, 1)
        write(j, 0)
        pick(jnp.minimum(j + 2, LEAF - 1), 0)
        write(j + 1, 1)
        return carry

    with jax.named_scope("pick_and_write"):
        lax.fori_loop(0, LEAF // 2, step, 0)
    with jax.named_scope("drain"):
        pltpu.make_async_copy(xout, x_hbm, out_sem).wait()
        move.wait()


def per_device(rhs_held, row_map, sep_rhs, sep_inverse, sep_parent, leaf_inverse, leaf_coupling, leaf_links):
    hbm = pl.BlockSpec(memory_space=pltpu.HBM)
    vmem = pltpu.VMEM
    came, pos, sep = pl.pallas_call(
        kernel,
        out_shape=(
            jax.ShapeDtypeStruct((DEV * PITCH, 128), F32),
            jax.ShapeDtypeStruct((24, 128), I32),
            jax.ShapeDtypeStruct((R, W), F32),
        ),
        in_specs=[hbm] * 7 + [pl.BlockSpec(memory_space=pltpu.SMEM)],
        out_specs=(hbm, hbm, hbm),
        scratch_shapes=[
            vmem((R, ROWS), F32),
            vmem((24, 128), I32),
            vmem((R, W), F32),
            vmem((W, W), F32),
            vmem((W, W), F32),
            vmem((LEAF, W, W), F32),
            vmem((LEAF * NCOUP, W, W), F32),
            vmem((ROWS, 128), F32),
            vmem((DEV * PITCH, 128), F32),
            vmem((2 * DEV * PITCH, 128), F32),
            vmem((ROWS // 2, 128), F32),
            vmem((ROWS, 128), F32),
            vmem((DEV * PITCH, 128), F32),
            vmem((LEVELS * R, W), F32),
            vmem((R, W), F32),
            vmem((R, W), F32),
            vmem((LEVELS, 2 * R, W), BF16),
            vmem((LEAF, R, W), F32),
            vmem((12 * 128, 256), BF16),
            vmem((12 * 128, 384), F32),
            vmem((128, 128), F32),
            vmem((24, 128), I32),
            vmem((48, 128), I32),
            pltpu.SMEM((24, 128), I32),
            pltpu.SMEM((48, 128), I32),
            pltpu.SemaphoreType.DMA((7,)),
            pltpu.SemaphoreType.DMA((4,)),
            pltpu.SemaphoreType.DMA((2,)),
            pltpu.SemaphoreType.DMA((PARTS,)),
            pltpu.SemaphoreType.DMA,
            pltpu.SemaphoreType.DMA((2,)),
            pltpu.SemaphoreType.DMA,
            pltpu.SemaphoreType.DMA((5,)),
            pltpu.SemaphoreType.DMA,
            pltpu.SemaphoreType.DMA,
            pltpu.SemaphoreType.DMA,
            pltpu.SemaphoreType.DMA,
            pltpu.SemaphoreType.DMA((2,)),
            pltpu.SemaphoreType.DMA((2,)),
            pltpu.SemaphoreType.DMA((2,)),
            pltpu.SemaphoreType.DMA,
            pltpu.SemaphoreType.DMA,
            pltpu.SemaphoreType.DMA,
            pltpu.SemaphoreType.DMA,
            pltpu.SemaphoreType.REGULAR,
        ],
        compiler_params=pltpu.CompilerParams(
            collective_id=0, has_side_effects=True, vmem_limit_bytes=56 << 20
        ),
        name="gmrf_solve",
    )(
        rhs_held.T,
        row_map.reshape(24, 128),
        sep_rhs[0].T,
        sep_inverse[0],
        sep_parent[0],
        leaf_inverse[0],
        leaf_coupling[0].reshape(LEAF * NCOUP, W, W),
        leaf_links[0].T,
    )
    x, sep = pl.pallas_call(
        restore_kernel,
        out_shape=(jax.ShapeDtypeStruct((R, ROWS), F32), jax.ShapeDtypeStruct((R, W), F32)),
        in_specs=[hbm, pl.BlockSpec(memory_space=pltpu.SMEM), hbm],
        out_specs=(hbm, hbm),
        scratch_shapes=[
            vmem((2 * DEV * PITCH, 128), F32),
            vmem((2, 128, 128), F32),
            vmem((R, ROWS), F32),
            pltpu.SemaphoreType.DMA((6,)),
            pltpu.SemaphoreType.DMA,
        ],
        compiler_params=pltpu.CompilerParams(vmem_limit_bytes=56 << 20),
        name="restore_rows",
    )(came, pos, sep)
    return x.T, sep.T[None]


def solution(mesh):
    in_specs = (
        P(("row", "col"), None),
        P(("row", "col")),
        P(("row", "col"), None, None),
        P(("row", "col"), None, None),
        P(("row", "col"), None, None),
        P(("row", "col"), None, None, None),
        P(("row", "col"), None, None, None, None),
        P(("row", "col"), None, None),
    )
    out_specs = (P(("row", "col"), None), P(("row", "col"), None, None))
    return jax.shard_map(per_device, mesh=mesh, in_specs=in_specs, out_specs=out_specs, check_vma=False)
```

```python
import functools

import jax
import jax.numpy as jnp
from jax import lax
from jax.experimental import pallas as pl
from jax.experimental.pallas import tpu as pltpu
from jax.sharding import PartitionSpec as P

MESH = pl.DeviceIdType.MESH
F32 = jnp.float32
BF16 = jnp.bfloat16
I32 = jnp.int32
NN = (((1,), (0,)), ((), ()))
NT = (((1,), (1,)), ((), ()))

DEV = 128
LEVELS = 7
W = 256
R = 64
LEAF = 12
NCOUP = 4
ROWS = 3072
SEG = 24
HALF = 12
MSG = HALF + 1
BLOCK_STEP = 12
LEAF_STEP = 12
SPREAD = 37
PARTS = 4
PART = R // PARTS
PITCH = 16


def mesh_id(device):
    return (lax.shift_right_logical(device, 4), device & 15)


def split(value):
    high = value.astype(BF16)
    return high, (value - high.astype(F32)).astype(BF16)


def pieces(x):
    high, low = split(x)
    return jnp.concatenate([high, low], 0), high


def dot3(x2, xh, weights, dims):
    wh, wl = split(weights)
    n = xh.shape[0]
    both = lax.dot_general(x2, wh, dims, preferred_element_type=F32)
    cross = lax.dot_general(xh, wl, dims, preferred_element_type=F32)
    return both[:n] + both[n:] + cross


def iota(shape, axis):
    return lax.broadcasted_iota(I32, shape, axis)


def within(index, size):
    return jnp.clip(index, 0, size - 1)


def onehot(mask):
    return jnp.where(mask, 1.0, 0.0)


def trailing_zeros(number):
    total = jnp.int32(0)
    for k in range(1, 8):
        total = total + jnp.where((number & ((1 << k) - 1)) == 0, 1, 0)
    return total


def gather_pairs(steps, source, table, first, second, store, lanes=range(128)):
    left = iota((1, 128), 1) < R

    def step(k, carry):
        for l in lanes:
            a = table[first(k), l]
            b = table[second(k), l]
            store(k, l, jnp.where(left, source[pl.ds(a, 1), :], source[pl.ds(b, 1), :]))
        return carry

    lax.fori_loop(0, steps, step, 0)


def swap_halves(both, first=0, count=DEV * PITCH):
    def group(g, carry):
        at = pl.multiple_of(first + g * 128, 128)
        both[pl.ds(at + DEV * PITCH, 128), :] = pltpu.roll(both[pl.ds(at, 128), :], R, 1)
        return carry

    lax.fori_loop(0, count // 128, group, 0, unroll=4)


def kernel(
    rhs_hbm, map_hbm, seprhs_hbm, sepinv_hbm, seppar_hbm, leafinv_hbm, coup_hbm, links,
    came_hbm, pos_hbm, sep_hbm,
    rhs, rmap, seprhs, sepinv, seppar, leafinv, coup,
    doubled, sbuf, received, grouped, solved, sbuf2,
    anc, crit, sepout, ready, acc, qt, cums, labels, pos_v, idx_v, idx, idx_r,
    in_sem, loc_sem, crit_send, crit_recv, part_recv, zero_send, zero_recv, four_send, four_recv, five_send, five_recv,
    scat_send, scat_recv, ag_send, ag_recv, a_send, a_recv, b_send, b_recv, gate,
):
    me = lax.axis_index("row") * 16 + lax.axis_index("col")

    loads = [
        pltpu.make_async_copy(s, d, in_sem.at[i])
        for i, (s, d) in enumerate(
            (
                (sepinv_hbm, sepinv), (seprhs_hbm, seprhs), (map_hbm, rmap), (seppar_hbm, seppar),
                (rhs_hbm, rhs), (coup_hbm, coup), (leafinv_hbm, leafinv),
            )
        )
    ]
    for load in loads:
        load.start()

    barrier = pltpu.get_barrier_semaphore()

    for k in [16 * i for i in range(1, 8)] + list(range(1, 16)):
        pl.semaphore_signal(barrier, inc=1, device_id=mesh_id(me ^ k), device_id_type=MESH)

    own = 6 - trailing_zeros(me + 1)
    reach = lax.shift_right_logical(jnp.int32(32), jnp.clip(own, 0, 5))
    inner = (own >= 0) & (own < 6)
    x_at = me & 3
    even = (me & 1) == 0

    def remote(src, dst, send, recv, to):
        return pltpu.make_async_remote_copy(
            src_ref=src, dst_ref=dst, send_sem=send, recv_sem=recv, device_id=mesh_id(to), device_id_type=MESH
        )

    def rows_of(first, count):
        return anc.at[pl.ds(pl.multiple_of(first, 8), count)]

    def drain(count, sem):
        pltpu.make_async_copy(anc.at[pl.ds(0, count)], anc.at[pl.ds(0, count)], sem).wait()

    def set_level(m, value):
        anc[m * R:(m + 1) * R, :] = value

    def send_part(h):
        part = pl.ds(h * PART, PART)

        @pl.when(inner)
        def _():
            remote(sepout.at[part], crit.at[part], crit_send.at[0], crit_recv.at[h], me - reach).start()
            remote(sepout.at[part], crit.at[part], crit_send.at[1], crit_recv.at[h], me + reach).start()

        @pl.when(own == 6)
        def _():
            remote(sepout.at[part], rows_of(6 * R + h * PART, PART), crit_send.at[0], part_recv, me + 1).start()

    def finish_children():
        drain(R, crit_send.at[0])
        drain(R, crit_send.at[1])

    def zero_to(to, which):
        return remote(crit, rows_of(0, R), zero_send.at[which], zero_recv, to)

    def four_to():
        return [
            remote(sepout, rows_of(4 * R, R), four_send.at[i], four_recv, (me & 120) | low)
            for i, low in enumerate((0, 2, 7, 4, 6))
        ]

    def five_to():
        return remote(sepout, rows_of(5 * R, R), five_send, five_recv, me + 2)

    def solve_part(h, target):
        t2, th = pieces(target)
        sepout[h * PART:(h + 1) * PART, :] = dot3(t2, th, sepinv[...], NT)

    def take_and_solve():
        for h in range(PARTS):
            rows = slice(h * PART, (h + 1) * PART)
            with jax.named_scope("parent_wait"):
                pltpu.make_async_copy(sepout.at[pl.ds(0, PART)], crit.at[pl.ds(0, PART)], crit_recv.at[h]).wait()
            with jax.named_scope("own_solve"):
                p2, ph = pieces(crit[rows, :])
                solve_part(h, seprhs[rows, :] - dot3(p2, ph, seppar[...], NN))
            send_part(h)

        @pl.when(own == 5)
        def _():
            five_to().start()

    def heard_first():
        pl.semaphore_wait(barrier, 22)

        for i in range(1, 8):
            pl.semaphore_signal(gate, inc=1, device_id=mesh_id(me ^ (16 * i)), device_id_type=MESH)

    loads[0].wait()
    loads[1].wait()

    @pl.when(own == 0)
    def _():
        for h in range(PARTS):
            solve_part(h, seprhs[h * PART:(h + 1) * PART, :])
        heard_first()
        for h in range(PARTS):
            send_part(h)

    @pl.when(own < 0)
    def _():
        sepout[...] = jnp.zeros_like(sepout)

    loads[2].wait()
    rows = rmap[...]
    dest = lax.shift_right_logical(lax.shift_right_logical(rows, 10) * 171, 9)
    local = rows - dest * ROWS
    for j in range(12):
        for h in range(2):
            r = 2 * j + h
            qt[j * 128:(j + 1) * 128, h * 128:(h + 1) * 128] = onehot(
                iota((128, 128), 0) == dest[r:r + 1, :]
            ).astype(BF16)
    tri = onehot((iota((256, 384), 0) < iota((256, 384), 1)) | (iota((256, 384), 1) >= 256)).astype(BF16)
    cums[...] = lax.dot_general(qt[...], tri, NN, preferred_element_type=F32)
    carry = jnp.zeros((128, 128), F32)
    table = jnp.zeros((128, 128), F32)
    sub32 = iota((32, 128), 0)
    lane = iota((1, 128), 1)
    for j in range(12):
        parts = []
        for h in range(2):
            r = 2 * j + h
            q = qt[j * 128:(j + 1) * 128, h * 128:(h + 1) * 128].astype(F32)
            rank = jnp.sum(q * (cums[j * 128:(j + 1) * 128, h * 128:(h + 1) * 128] + carry), axis=0, keepdims=True)
            rank = rank.astype(I32)
            hit = sub32 == rank
            loc = local[r:r + 1, :]
            parts.append(
                jnp.concatenate(
                    [
                        jnp.where(hit, float(r), 0.0),
                        jnp.where(hit, lane.astype(F32), 0.0),
                        jnp.where(hit, lax.shift_right_logical(loc, 7).astype(F32), 0.0),
                        jnp.where(hit, (loc & 127).astype(F32), 0.0),
                    ],
                    0,
                )
            )
            at = dest[r:r + 1, :] * PITCH + rank + jnp.where(rank >= HALF, DEV * PITCH - HALF, 0)
            pos_v[r:r + 1, :] = within(at, 2 * DEV * PITCH) ^ (h * DEV * PITCH)
        digits = jnp.concatenate(parts, 1).astype(BF16)
        table = table + lax.dot_general(digits, qt[j * 128:(j + 1) * 128, :], NT, preferred_element_type=F32)
        carry = carry + cums[j * 128:(j + 1) * 128, 256:384]
    idx_v[0:24, :] = within((table[0:24] * 128.0 + table[32:56]).astype(I32), ROWS)
    to_idx = pltpu.make_async_copy(idx_v.at[pl.ds(0, 24)], idx, loc_sem.at[0])
    to_idx.start()
    to_pos = pltpu.make_async_copy(pos_v, pos_hbm, loc_sem.at[1])
    to_pos.start()
    lab = table[64:96] * 128.0 + table[96:128]
    labels[...] = jnp.concatenate([lab, jnp.zeros((96, 128), F32)], 0).T

    loads[4].wait()

    def double_rhs(j, carry):
        block = rhs[:, pl.ds(pl.multiple_of(j * 128, 128), 128)]
        doubled[pl.ds(pl.multiple_of(j * 128, 128), 128), :] = jnp.concatenate([block, block], 0).T
        return carry

    lax.fori_loop(0, ROWS // 128, double_rhs, 0, unroll=12)

    to_idx.wait()

    def put_send(k, l, row):
        sbuf[pl.ds(l * PITCH + k, 1), :] = row

    def landing(dst, device, n):
        return dst.at[pl.ds(pl.multiple_of(device * PITCH, PITCH), n)]

    def exchange(core, src, dst, n, send, recv):
        def send_one(k):
            j = (k * SPREAD) & 63
            to = (me ^ ((j & 15) + (j // 16) * 32)) & 111 | (core * 16)
            remote(landing(src, to, n), landing(dst, me, n), send, recv, to).start()

        @pl.when((lax.shift_right_logical(me, 4) & 1) != core)
        def _():
            send_one(0)

        def go(k, carry):
            send_one(k)
            return carry

        lax.fori_loop(1, 64, go, 0, unroll=1)

    def lanes_of(core):
        return [l for l in range(DEV) if (l >> 4) & 1 == core]

    def exchange_wait(rows, n, sem):
        count = (DEV - 1) * n
        pltpu.make_async_copy(rows.at[pl.ds(0, count)], rows.at[pl.ds(0, count)], sem).wait()

    @pl.when(own != 0)
    def _():
        heard_first()

    loads[3].wait()

    @pl.when(own == 1)
    def _():
        take_and_solve()
        zero_to(me - reach, 0).start()
        zero_to(me + reach, 1).start()

    gather_pairs(HALF, doubled, idx, lambda k: k, lambda k: k + HALF, put_send)
    for l in range(DEV):
        sbuf[l * PITCH + HALF:l * PITCH + MSG, :] = labels[l:l + 1, :]
    pl.semaphore_wait(gate, 7)

    @pl.when(own == 0)
    def _():
        finish_children()

    @pl.when(own == 2)
    def _():
        take_and_solve()

    @pl.when(own == 2)
    def _():
        set_level(1, crit[...])
        set_level(2, sepout[...])
        drain(R, zero_recv)

        def tile(i, carry):
            to = (me & 96) | (i // 3 * 4 + i % 3)
            remote(rows_of(i * 8, 8), rows_of(i * 8, 8), scat_send, scat_recv.at[0], to).start()
            return carry

        lax.fori_loop(0, 24, tile, 0)

    for core in range(2):
        exchange(core, sbuf, received, MSG, a_send, a_recv)
    keep = pltpu.make_async_copy(landing(sbuf, me, MSG), landing(received, me, MSG), loc_sem.at[2])
    keep.start()

    @pl.when(own == 3)
    def _():
        take_and_solve()
        set_level(3, sepout[...])
        for i in range(8):
            part = rows_of(3 * R + 8 * i, 8)
            remote(part, part, scat_send, scat_recv.at[1], (me & 112) | (i // 2 * 4 + i % 2 * 2)).start()

    @pl.when(own == 4)
    def _():
        take_and_solve()
        set_level(4, sepout[...])
        finish_children()
        for c in four_to():
            c.start()

    @pl.when(x_at != 3)
    def _():
        drain(8, scat_recv.at[0])
        part = rows_of((lax.shift_right_logical(me, 2) & 7) * 24 + x_at * 8, 8)

        def hand(k, carry):
            to = me ^ k

            @pl.when((to & 31) != 15)
            def _():
                remote(part, part, ag_send.at[0], ag_recv.at[0], to).start()

            return carry

        lax.fori_loop(1, 32, hand, 0)

    exchange_wait(doubled, MSG, a_recv)
    keep.wait()
    for p in range(128):
        labels[p:p + 1, :] = received[p * PITCH + HALF:p * PITCH + MSG, :]
    got = labels[...].T[0:32].astype(I32)
    high = lax.shift_right_logical(got, 7)
    low = got & 127
    inverse = jnp.zeros((64, 128), F32)
    for j in range(12):
        aa, bb = [], []
        for h in range(2):
            r = 2 * j + h
            at = lane * PITCH + (r % HALF + (r // HALF) * DEV * PITCH)
            hit = sub32 == high[r:r + 1, :]
            aa.append(
                jnp.concatenate(
                    [
                        jnp.where(hit, lax.shift_right_logical(at, 6).astype(F32), 0.0),
                        jnp.where(hit, (at & 63).astype(F32), 0.0),
                    ],
                    0,
                )
            )
            bb.append(onehot(iota((128, 128), 0) == low[r:r + 1, :]))
        inverse = inverse + lax.dot_general(
            jnp.concatenate(aa, 1).astype(BF16), jnp.concatenate(bb, 1).astype(BF16), NT, preferred_element_type=F32
        )
    found_at = within((inverse[0:24] * 64.0 + inverse[32:56]).astype(I32), 2 * DEV * PITCH)
    idx_v[0:24, :] = found_at ^ ((iota((24, 128), 0) & 1) * (DEV * PITCH))
    idx_v[24:48, :] = within(((high & 1) * (ROWS // 2) + lax.shift_right_logical(high, 1) * 128 + low)[0:24], ROWS)
    to_idx = pltpu.make_async_copy(idx_v, idx_r, loc_sem.at[0])
    to_idx.start()

    swap_halves(received)
    @pl.when(own == 5)
    def _():
        take_and_solve()
        set_level(4, crit[...])
        set_level(5, sepout[...])

    @pl.when(even)
    def _():
        drain(8, scat_recv.at[1])
        part = rows_of(3 * R + (lax.shift_right_logical(me, 2) & 3) * 16 + x_at * 4, 8)

        def hand(k, carry):
            to = me ^ k

            @pl.when((to & 15) != 7)
            def _():
                remote(part, part, ag_send.at[1], ag_recv.at[1], to).start()

            return carry

        lax.fori_loop(1, 16, hand, 0)

    to_idx.wait()

    def put_grouped(k, l, row):
        grouped[pl.ds(k * 128 + l, 1), :] = row

    gather_pairs(LEAF, received, idx_r, lambda k: 2 * k, lambda k: 2 * k + 1, put_grouped)

    @pl.when(own == 6)
    def _():
        take_and_solve()
        set_level(5, crit[...])
        set_level(6, sepout[...])

    loads[5].wait()

    def make_ready(m):
        x2, _ = pieces(anc[m * R:(m + 1) * R, :])
        ready[m] = x2

    def block(i):
        def blocks(g, carry):
            for u in range(BLOCK_STEP):
                s = g * BLOCK_STEP + u
                link = [links[c, s] for c in range(NCOUP)]
                which = jnp.int32(0)
                level = jnp.int32(0)
                for c in range(NCOUP):
                    above = jnp.int32(0)
                    for other in range(NCOUP):
                        if other != c:
                            above = above + jnp.where(link[other] > link[c], 1, 0)
                    which = jnp.where(above == i, c, which)
                    level = jnp.where(above == i, LEVELS - 1 - link[c], level)
                x2 = ready[level]
                term = dot3(x2, x2[:R], coup[s * NCOUP + which], NN)
                acc[s] = term if i == 0 else acc[s] + term
            return carry

        lax.fori_loop(0, LEAF // BLOCK_STEP, blocks, 0)

    @pl.when((x_at != 3))
    def _():
        drain(184, ag_recv.at[0])

    @pl.when((x_at == 3) & (own != 2))
    def _():
        drain(192, ag_recv.at[0])

    @pl.when(even)
    def _():
        drain(56, ag_recv.at[1])

    @pl.when(~even & ((me & 15) != 7))
    def _():
        drain(64, ag_recv.at[1])

    for m in range(4):
        make_ready(m)
    block(0)

    @pl.when(even | ((me & 7) == 7))
    def _():
        drain(R, four_recv)

    make_ready(4)
    block(1)

    @pl.when(x_at == 3)
    def _():
        drain(R, five_recv)

    make_ready(5)
    block(2)

    @pl.when(~even)
    def _():
        drain(R, part_recv)

    make_ready(6)
    block(3)

    loads[6].wait()

    def leaf(g, carry):
        for u in range(LEAF_STEP):
            t = g * LEAF_STEP + u
            at = pl.multiple_of(t * 128, 128)
            both = grouped[pl.ds(at, 128), :].T
            target = jnp.concatenate([both[:R], both[R:]], 1) - acc[t]
            t2, th = pieces(target)
            x = dot3(t2, th, leafinv[t], NT)
            solved[pl.ds(at, 128), :] = jnp.concatenate([x[:, :128], x[:, :128]], 0).T
            solved[pl.ds(pl.multiple_of(at + ROWS // 2, 128), 128), :] = jnp.concatenate([x[:, 128:], x[:, 128:]], 0).T
        return carry

    lax.fori_loop(0, LEAF // LEAF_STEP, leaf, 0)

    def put_back(k, l, row):
        sbuf2[pl.ds(l * PITCH + k, 1), :] = row

    for core in range(2):
        gather_pairs(HALF, solved, idx_r, lambda k: k + 24, lambda k: k + 24 + HALF, put_back, lanes_of(core))
        exchange(core, sbuf2, came_hbm, HALF, b_send, b_recv)
    mine = pltpu.make_async_copy(landing(sbuf2, me, HALF), landing(came_hbm, me, HALF), loc_sem.at[2])
    mine.start()
    out_sep = pltpu.make_async_copy(sepout, sep_hbm, loc_sem.at[3])
    out_sep.start()

    exchange_wait(doubled, MSG, a_send)

    @pl.when(own == 6)
    def _():
        drain(R, crit_send.at[0])

    @pl.when(own == 5)
    def _():
        five_to().wait_send()

    @pl.when(((own >= 1) & (own <= 3)) | (own == 5))
    def _():
        finish_children()

    @pl.when(own == 1)
    def _():
        zero_to(me - reach, 0).wait_send()
        zero_to(me + reach, 1).wait_send()

    @pl.when(own == 2)
    def _():
        drain(192, scat_send)

    @pl.when(own == 3)
    def _():
        drain(64, scat_send)

    @pl.when(own == 4)
    def _():
        for c in four_to():
            c.wait_send()

    @pl.when(x_at != 3)
    def _():
        drain(240, ag_send.at[0])

    @pl.when(even)
    def _():
        drain(112, ag_send.at[1])

    to_pos.wait()
    out_sep.wait()
    mine.wait()
    exchange_wait(doubled, HALF, b_recv)
    exchange_wait(doubled, HALF, b_send)


def restore_kernel(came_hbm, pos, sep_hbm, x_hbm, sepx_hbm, came, grouped, xout, sem, out_sem):
    part = DEV * PITCH // 4
    loads = [
        pltpu.make_async_copy(came_hbm.at[pl.ds(i * part, part)], came.at[pl.ds(i * part, part)], sem.at[2 + i])
        for i in range(4)
    ]
    for load in loads:
        load.start()
    move = pltpu.make_async_copy(sep_hbm, sepx_hbm, sem.at[1])
    move.start()
    with jax.named_scope("load_and_swap"):
        for i in range(4):
            loads[i].wait()
            swap_halves(came, i * part, part)
    left = iota((1, 128), 1) < R

    def pick(j, slot):
        for l in range(128):
            a = pos[2 * j, l]
            b = pos[2 * j + 1, l]
            grouped[slot, l:l + 1, :] = jnp.where(left, came[pl.ds(a, 1), :], came[pl.ds(b, 1), :])

    def write(j, slot):
        at = pl.ds(pl.multiple_of(j * 256, 256), 256)
        both = grouped[slot].T
        xout[:, at] = jnp.concatenate([both[:R], both[R:]], 1)
        pltpu.make_async_copy(xout.at[:, at], x_hbm.at[:, at], out_sem).start()

    with jax.named_scope("pick_first"):
        pick(0, 0)

    def step(i, carry):
        j = 2 * i
        pick(j + 1, 1)
        write(j, 0)
        pick(jnp.minimum(j + 2, LEAF - 1), 0)
        write(j + 1, 1)
        return carry

    with jax.named_scope("pick_and_write"):
        lax.fori_loop(0, LEAF // 2, step, 0)
    with jax.named_scope("drain"):
        pltpu.make_async_copy(xout, x_hbm, out_sem).wait()
        move.wait()


def per_device(rhs_held, row_map, sep_rhs, sep_inverse, sep_parent, leaf_inverse, leaf_coupling, leaf_links):
    hbm = pl.BlockSpec(memory_space=pltpu.HBM)
    vmem = pltpu.VMEM
    came, pos, sep = pl.pallas_call(
        kernel,
        out_shape=(
            jax.ShapeDtypeStruct((DEV * PITCH, 128), F32),
            jax.ShapeDtypeStruct((24, 128), I32),
            jax.ShapeDtypeStruct((R, W), F32),
        ),
        in_specs=[hbm] * 7 + [pl.BlockSpec(memory_space=pltpu.SMEM)],
        out_specs=(hbm, hbm, hbm),
        scratch_shapes=[
            vmem((R, ROWS), F32),
            vmem((24, 128), I32),
            vmem((R, W), F32),
            vmem((W, W), F32),
            vmem((W, W), F32),
            vmem((LEAF, W, W), F32),
            vmem((LEAF * NCOUP, W, W), F32),
            vmem((ROWS, 128), F32),
            vmem((DEV * PITCH, 128), F32),
            vmem((2 * DEV * PITCH, 128), F32),
            vmem((ROWS // 2, 128), F32),
            vmem((ROWS, 128), F32),
            vmem((DEV * PITCH, 128), F32),
            vmem((LEVELS * R, W), F32),
            vmem((R, W), F32),
            vmem((R, W), F32),
            vmem((LEVELS, 2 * R, W), BF16),
            vmem((LEAF, R, W), F32),
            vmem((12 * 128, 256), BF16),
            vmem((12 * 128, 384), F32),
            vmem((128, 128), F32),
            vmem((24, 128), I32),
            vmem((48, 128), I32),
            pltpu.SMEM((24, 128), I32),
            pltpu.SMEM((48, 128), I32),
            pltpu.SemaphoreType.DMA((7,)),
            pltpu.SemaphoreType.DMA((4,)),
            pltpu.SemaphoreType.DMA((2,)),
            pltpu.SemaphoreType.DMA((PARTS,)),
            pltpu.SemaphoreType.DMA,
            pltpu.SemaphoreType.DMA((2,)),
            pltpu.SemaphoreType.DMA,
            pltpu.SemaphoreType.DMA((5,)),
            pltpu.SemaphoreType.DMA,
            pltpu.SemaphoreType.DMA,
            pltpu.SemaphoreType.DMA,
            pltpu.SemaphoreType.DMA,
            pltpu.SemaphoreType.DMA((2,)),
            pltpu.SemaphoreType.DMA((2,)),
            pltpu.SemaphoreType.DMA((2,)),
            pltpu.SemaphoreType.DMA,
            pltpu.SemaphoreType.DMA,
            pltpu.SemaphoreType.DMA,
            pltpu.SemaphoreType.DMA,
            pltpu.SemaphoreType.REGULAR,
        ],
        compiler_params=pltpu.CompilerParams(
            collective_id=0, has_side_effects=True, vmem_limit_bytes=56 << 20
        ),
        name="gmrf_solve",
    )(
        rhs_held.T,
        row_map.reshape(24, 128),
        sep_rhs[0].T,
        sep_inverse[0],
        sep_parent[0],
        leaf_inverse[0],
        leaf_coupling[0].reshape(LEAF * NCOUP, W, W),
        leaf_links[0].T,
    )
    x, sep = pl.pallas_call(
        restore_kernel,
        out_shape=(jax.ShapeDtypeStruct((R, ROWS), F32), jax.ShapeDtypeStruct((R, W), F32)),
        in_specs=[hbm, pl.BlockSpec(memory_space=pltpu.SMEM), hbm],
        out_specs=(hbm, hbm),
        scratch_shapes=[
            vmem((2 * DEV * PITCH, 128), F32),
            vmem((2, 128, 128), F32),
            vmem((R, ROWS), F32),
            pltpu.SemaphoreType.DMA((6,)),
            pltpu.SemaphoreType.DMA,
        ],
        compiler_params=pltpu.CompilerParams(vmem_limit_bytes=56 << 20),
        name="restore_rows",
    )(came, pos, sep)
    return x.T, sep.T[None]


def solution(mesh):
    in_specs = (
        P(("row", "col"), None),
        P(("row", "col")),
        P(("row", "col"), None, None),
        P(("row", "col"), None, None),
        P(("row", "col"), None, None),
        P(("row", "col"), None, None, None),
        P(("row", "col"), None, None, None, None),
        P(("row", "col"), None, None),
    )
    out_specs = (P(("row", "col"), None), P(("row", "col"), None, None))
    return jax.shard_map(per_device, mesh=mesh, in_specs=in_specs, out_specs=out_specs, check_vma=False)
```
